32 devices in a mesh: grp: 4 (over y, x), row: 8 (over z, core).
Axes of the slice: x: 2, y: 2, z: 4, core: 2. Of those that a mesh axis runs over, the one named last changes fastest.
Arguments:
- green: bfloat16 [8192, 8192], P('grp', 'row'), may hold values from -0.5 to 0.5
- footprint: int32 [64, 64], P('grp', 'row'), may hold values from 0 to 1, as said below
- set_index: int32 [64], P('grp'), may hold values from 0 to 7
- set_weight: float32 [8], replicated, may hold values from 0.3 to 3
- pixel_scale: float32 [8192], P('grp'), may hold values from 0.1 to 1
- panel_index: int32 [1], replicated, may hold values from 0 to 15
Outputs:
- gram_panel: float32 [8192, 512], P(('row', 'grp'))
The draws below stay inside these ranges and needn't reach their ends.
Inputs may be any that keep to these rules, and one draw needn't show every extreme that they name: `footprint`: each entry is 0 or 1; how dense a column of blocks is varies between unknown blocks.
All inputs are finite; a program needn't handle non-finite values.
Results may differ from the reference program's by a relative error of at most 0.0026.
Values may be sent and summed in bfloat16 or wider, within the bound.
No kernel may reach another device: no remote copies, remote signals or barrier semaphores. Data moves between devices by JAX's collectives and lax.ppermute only.
A program may use at most 64 MiB of HBM per device.

```python
import math
import jax
import jax.numpy as jnp
from jax import lax

B = 128
PANEL = 4
NSETS = 8
PB_G = 16
NPB = 64
PIX = 8192
NBLK = 64
UNK = 8192
N_GRP = 4


def draw_footprint(key, part):
    level_key = jax.random.fold_in(key, 11)
    value_key = jax.random.fold_in(key, 12)
    level = jax.random.randint(level_key, (1, NBLK), 1, 8)
    value = jax.random.randint(value_key, (NPB, NBLK), 0, 8)
    return (value < level).astype(jnp.int32)


def with_ends(array, own_key, smallest, high):
    longest = array.shape.index(max(array.shape))
    spots = []
    for shift in (0, 1):
        where = [jax.random.randint(jax.random.fold_in(own_key, axis), (), 0, length) for axis, length in enumerate(array.shape)]
        where[longest] = (where[longest] + shift) % array.shape[longest]
        spots.append(tuple(where))
    return array.at[spots[0]].set(smallest).at[spots[1]].set(high)


def raised(result, key, source, target, blocks, factor):
    def block_of(dim):
        return (jnp.arange(result.shape[dim]) // (result.shape[dim] // blocks)).reshape((-1,) + (1,) * (result.ndim - 1 - dim))

    one_side = jax.random.permutation(key, blocks)[block_of(target)]
    second = (block_of(target) + blocks // 2) % blocks
    return jnp.where((block_of(source) == one_side) | (block_of(source) == second), factor * result, result)


def level_of(key, shape, split, least, high):
    def one(dim, blocks):
        steps = jax.random.uniform(jax.random.fold_in(jax.random.fold_in(key, 6), dim), (blocks,), jnp.float32, least / len(split), high / len(split))
        return jnp.repeat(jnp.exp(steps), shape[dim] // blocks).reshape((-1,) + (1,) * (len(shape) - dim - 1))

    factor_of = one(*split[0])
    for cut in split[1:]:
        factor_of = factor_of * one(*cut)
    return factor_of


def noise_with(rng, extent, deviation, bound, pieces, heavy, kind=jnp.bfloat16):
    values = deviation * jax.random.normal(rng, extent, jnp.float32)
    if pieces:
        values = values * level_of(rng, extent, pieces, -0.22, 0.18)
    return jnp.clip(raised(values, jax.random.fold_in(rng, 3), *heavy), -bound, bound).astype(kind)


def setup_inputs(seed: int = 0) -> dict:
    seeds = jax.random.split(jax.random.key(seed), 7)
    green = noise_with(seeds[0], (PIX, UNK), (2 * B) ** -0.5, 0.5, ((0, 4), (1, 8)), (0, 1, 8, 2.0))
    footprint = draw_footprint(jax.random.fold_in(seeds[6], 71), 0)
    set_index = with_ends(jax.random.randint(seeds[2], (NPB,), 0, NSETS), jax.random.fold_in(seeds[2], 1), 0, NSETS - 1).astype(jnp.int32)
    set_weight = jnp.clip(jnp.exp(jax.random.uniform(seeds[3], (NSETS,), jnp.float32, math.log(0.3), math.log(3.0))), 0.3, 3.0)
    pixel_scale = jnp.clip(jnp.exp(math.log(1.0) - 2.3025851 * jax.random.uniform(seeds[4], (PIX,), jnp.float32) ** level_of(seeds[4], (PIX,), ((0, 4),), -0.2, 0.2)), 0.1, 1.0)
    panel_index = jax.random.randint(seeds[5], (1,), 0, NBLK // PANEL).astype(jnp.int32)
    return {"green": green, "footprint": footprint, "set_index": set_index, "set_weight": set_weight, "pixel_scale": pixel_scale, "panel_index": panel_index}


def reference(green, footprint, set_index, set_weight, pixel_scale, panel_index):
    first = (panel_index[0] * PANEL).astype(jnp.int32)
    mask_cols = lax.dynamic_slice_in_dim(footprint, first, PANEL, 1).astype(jnp.bfloat16)
    panel = lax.dynamic_slice_in_dim(green, first * B, PANEL * B, 1)
    panel = (panel.reshape(NPB, B, PANEL, B) * mask_cols[:, None, :, None]).reshape(PIX, PANEL * B)
    onehot = (set_index[:, None] == jnp.arange(NSETS, dtype=jnp.int32)[None, :]).astype(jnp.float32)
    block_weight = jnp.sum(onehot * set_weight[None, :], axis=1)
    weight = (pixel_scale.reshape(NPB, B) * block_weight[:, None]).reshape(PIX)
    weighted = (panel.astype(jnp.float32) * weight[:, None]).astype(jnp.bfloat16)
    fmask = footprint.astype(jnp.bfloat16)

    def one_group(index, total):
        start = (index * PB_G).astype(jnp.int32)
        rows = lax.dynamic_slice_in_dim(green, start * B, PB_G * B, 0)
        mrows = lax.dynamic_slice_in_dim(fmask, start, PB_G, 0)
        masked = (rows.reshape(PB_G, B, NBLK, B) * mrows[:, None, :, None]).reshape(PB_G * B, UNK)
        wrows = lax.dynamic_slice_in_dim(weighted, start * B, PB_G * B, 0)
        return total + lax.dot_general(masked, wrows, (((0,), (0,)), ((), ())), preferred_element_type=jnp.float32)

    return lax.fori_loop(0, N_GRP, one_group, jnp.zeros((UNK, PANEL * B), jnp.float32))
```

```python
import functools
import jax
import jax.numpy as jnp
from jax import lax
from jax.experimental import pallas as pl
from jax.experimental.pallas import tpu as pltpu
from jax.sharding import PartitionSpec as P

PANEL = 4
VMEM_LIMIT = 48 * 1024 * 1024


def whole_vmem():
    return pl.BlockSpec(memory_space=pltpu.VMEM)


def smem():
    return pl.BlockSpec(memory_space=pltpu.SMEM)


def spread(owner, chips):
    levels = {}

    def serve(source, run, depth):
        if not run:
            return
        middle = run[len(run) // 2] if len(run) > 2 else run[0]
        levels.setdefault(depth, []).append((source, middle))
        at = run.index(middle)
        serve(middle, run[:at][::-1], depth + 1)
        serve(middle, run[at + 1 :], depth + 1)

    serve(owner, list(range(owner + 1, chips)), 0)
    serve(owner, list(range(owner - 1, -1, -1)), 0)
    rounds = []
    for depth in sorted(levels):
        left = levels[depth]
        while left:
            used, later, now = set(), [], []
            for edge in left:
                (later if edge[0] in used else now).append(edge)
                used.add(edge[0])
            rounds.append(now)
            left = later
    return rounds


def prep_body(cols, blocks, half_blocks, width, meta, panel_ref, fp_ref, set_ref, sw_ref, *refs):
    scales, greens, outs = refs[:2], refs[2 : 2 + 2 * len(cols)], refs[2 + 2 * len(cols) :]
    first = lax.rem(panel_ref[0] * PANEL, blocks)
    for side in range(2):
        half = meta[0] if side == 0 else 1 - meta[0]
        for i in range(half_blocks):
            at = half * half_blocks + i
            weight = scales[side][i : i + 1, :] * sw_ref[set_ref[at]]
            spread_weight = jnp.broadcast_to(weight, (width, width)).T
            for n, col in enumerate(cols):
                block = greens[2 * n + side][i * width : (i + 1) * width, :]
                value = (block.astype(jnp.float32) * spread_weight).astype(jnp.bfloat16)
                keep = fp_ref[at, first + col] != 0
                outs[2 * n + side][i * width : (i + 1) * width, :] = jnp.where(keep, value, jnp.zeros_like(value))


def prep(cols, meta, panel_index, footprint, set_index, set_weight, scale, green):
    rows = green.shape[0]
    pblocks, blocks = footprint.shape
    width = rows // pblocks
    half_blocks, half = pblocks // 2, rows // 2
    per = blocks // PANEL

    def green_spec(col, side):
        def where(_, m, p):
            return (m[0] if side == 0 else 1 - m[0], lax.rem(p[0], per) * PANEL + col)

        return pl.BlockSpec((half, width), where)

    def scale_spec(side):
        return pl.BlockSpec((half_blocks, width), lambda _, m, p: (m[0] if side == 0 else 1 - m[0], 0))

    shape = jax.ShapeDtypeStruct((half, width), jnp.bfloat16)
    return pl.pallas_call(
        functools.partial(prep_body, cols, blocks, half_blocks, width),
        grid_spec=pltpu.PrefetchScalarGridSpec(
            num_scalar_prefetch=2,
            grid=(1,),
            in_specs=[smem(), smem(), smem(), scale_spec(0), scale_spec(1)]
            + [green_spec(col, side) for col in cols for side in range(2)],
            out_specs=[pl.BlockSpec((half, width), lambda _, m, p: (0, 0))] * (2 * len(cols)),
        ),
        out_shape=[shape] * (2 * len(cols)),
        compiler_params=pltpu.CompilerParams(vmem_limit_bytes=VMEM_LIMIT),
        name="weigh_panel",
    )(meta, panel_index, footprint, set_index, set_weight, scale, scale, *([green] * (2 * len(cols))))


def turn_body(blocks, width, step_blocks, fp_ref, green_ref, out_ref):
    step = pl.program_id(0)
    for i in range(step_blocks):
        for j in range(blocks):
            block = green_ref[i * width : (i + 1) * width, j * width : (j + 1) * width]
            keep = fp_ref[step * step_blocks + i, j] != 0
            block = jnp.where(keep, block, jnp.zeros_like(block))
            out_ref[j * width : (j + 1) * width, i * width : (i + 1) * width] = block.T


def turn(footprint, green):
    rows, cols = green.shape
    pblocks, blocks = footprint.shape
    width = rows // pblocks
    steps = 4
    return pl.pallas_call(
        functools.partial(turn_body, blocks, width, pblocks // steps),
        grid=(steps,),
        in_specs=[smem(), pl.BlockSpec((rows // steps, cols), lambda i: (i, 0))],
        out_specs=pl.BlockSpec((cols, rows // steps), lambda i: (0, i)),
        out_shape=jax.ShapeDtypeStruct((cols, rows), jnp.bfloat16),
        compiler_params=pltpu.CompilerParams(vmem_limit_bytes=VMEM_LIMIT),
        name="mask_and_turn",
    )(footprint, green)


def gram_body(shares, meta, mine_ref, other_ref, turned_ref, *outs):
    core, group = meta[0], meta[1]
    half = mine_ref.shape[0]
    share = turned_ref.shape[0] // shares
    left = pl.ds(pl.multiple_of(core * half, half), half)
    right = pl.ds(pl.multiple_of((1 - core) * half, half), half)
    for s in range(shares):
        at = pl.ds(pl.multiple_of((group ^ s) * share, share), share)
        total = jnp.dot(turned_ref[at, left], mine_ref[...], preferred_element_type=jnp.float32)
        total += jnp.dot(turned_ref[at, right], other_ref[...], preferred_element_type=jnp.float32)
        outs[s][...] = total.astype(outs[s].dtype)


def gram(shares, meta, mine, other, turned):
    share, wide = turned.shape[0] // shares, mine.shape[1]
    return pl.pallas_call(
        functools.partial(gram_body, shares),
        in_specs=[smem(), whole_vmem(), whole_vmem(), whole_vmem()],
        out_specs=[whole_vmem()] * shares,
        out_shape=[jax.ShapeDtypeStruct((share, wide), jnp.float32 if s == 0 else jnp.bfloat16) for s in range(shares)],
        compiler_params=pltpu.CompilerParams(vmem_limit_bytes=VMEM_LIMIT),
        name="partial_gram",
    )(meta, mine, other, turned)


def sum_body(shares, *refs):
    out_ref = refs[-1]
    parts = refs[:-1]
    wide = parts[0].shape[1]
    for k in range(len(parts) // shares):
        total = parts[k * shares][...]
        for s in range(1, shares):
            total += parts[k * shares + s][...].astype(jnp.float32)
        out_ref[:, k * wide : (k + 1) * wide] = total


def total_of(shares, parts, panel_cols):
    return pl.pallas_call(
        functools.partial(sum_body, shares),
        in_specs=[whole_vmem()] * len(parts),
        out_specs=whole_vmem(),
        out_shape=jax.ShapeDtypeStruct((parts[0].shape[0], panel_cols), jnp.float32),
        compiler_params=pltpu.CompilerParams(vmem_limit_bytes=VMEM_LIMIT),
        name="sum_groups",
    )(*parts)


def on_device(groups, lanes, green, footprint, set_index, set_weight, pixel_scale, panel_index):
    rows, cols = green.shape
    pblocks, blocks = footprint.shape
    width = rows // pblocks
    chips = lanes // 2
    wide = 1 if chips <= 4 else PANEL
    row = lax.axis_index("row")
    core, chip = row & 1, row >> 1
    group = lax.axis_index("grp")
    meta = jnp.stack([core, group])
    owner = (panel_index[0] * PANEL) // blocks
    swap = [(r, r ^ 1) for r in range(lanes)]
    scale = pixel_scale.reshape(pblocks, width)
    chunks = [list(range(k, k + wide)) for k in range(0, PANEL, wide)]
    small = (meta, panel_index, footprint, set_index, set_weight, scale, green)

    def from_chip(source):
        def run(*small):
            meta, footprint, green = small[0], small[2], small[6]
            rounds = spread(source, chips)
            weighed = prep(chunks[0], *small)
            if len(chunks) > 1:
                weighed += prep([c for chunk in chunks[1:] for c in chunk], *small)
            parts = []
            turned = None
            for k in range(len(chunks)):
                pairs = weighed[2 * wide * k : 2 * wide * (k + 1)]
                own = jnp.concatenate(pairs[0::2], 1) if wide > 1 else pairs[0]
                away = jnp.concatenate(pairs[1::2], 1) if wide > 1 else pairs[1]
                start = jnp.where(row == owner, own, lax.ppermute(away, "row", swap))
                got = {source: start}
                mine = start
                for edges in rounds:
                    came = functools.reduce(
                        lambda v, e: v if e[0] == edges[0][0] else jnp.where(chip == e[0], got[e[0]], v),
                        edges,
                        got[edges[0][0]],
                    )
                    came = lax.ppermute(came, "row", [(2 * a + c, 2 * b + c) for a, b in edges for c in range(2)])
                    for _, b in edges:
                        got[b] = came
                        mine = jnp.where(chip == b, came, mine)
                other = lax.ppermute(mine, "row", swap)
                if turned is None:
                    turned = turn(footprint, green)
                pieces = gram(groups, meta, mine, other, turned)
                parts.append(pieces[0])
                for s in range(1, groups):
                    parts.append(lax.ppermute(pieces[s], "grp", [(g, g ^ s) for g in range(groups)]))
            return total_of(groups, parts, PANEL * width)

        return run

    return lax.switch(owner >> 1, [from_chip(source) for source in range(chips)], *small)


def solution(mesh):
    in_specs = (P("grp", "row"), P("grp", "row"), P("grp"), P(), P("grp"), P())
    out_specs = P(("row", "grp"), None)
    body = functools.partial(on_device, mesh.shape["grp"], mesh.shape["row"])
    return jax.shard_map(body, mesh=mesh, in_specs=in_specs, out_specs=out_specs, check_vma=False)
```

```python
import functools
import jax
import jax.numpy as jnp
from jax import lax
from jax.experimental import pallas as pl
from jax.experimental.pallas import tpu as pltpu
from jax.sharding import PartitionSpec as P

PANEL = 4
CHUNKS = ((0,), (1,), (2,), (3,))
BATCHES = ((0, 1), (2, 3))
TIE = 1
VMEM_LIMIT = 24 * 1024 * 1024
PREP_LIMIT = 60 * 1024 * 1024


def whole_vmem():
    return pl.BlockSpec(memory_space=pltpu.VMEM)


def smem():
    return pl.BlockSpec(memory_space=pltpu.SMEM)


def prep_body(chunks, lane, width, panel, fp_hbm, set_hbm, sw_hbm, scale_hbm, green_hbm, *refs):
    outs, (fp, sets, sw, scale, green, sems) = refs[: 2 * len(chunks)], refs[2 * len(chunks) :]
    blocks, pblocks = fp_hbm.shape
    half_blocks = pblocks // 2
    half = half_blocks * width
    low = chunks[0][0]
    first = lax.rem(panel[0] * PANEL, blocks)
    at = pl.ds(pl.multiple_of((first + low) * width, width), green.shape[1])
    copies = [
        pltpu.make_async_copy(source, target, sems.at[n])
        for n, (source, target) in enumerate(
            ((fp_hbm, fp), (set_hbm, sets), (sw_hbm, sw), (scale_hbm, scale), (green_hbm.at[:, at], green))
        )
    ]
    for copy in copies:
        copy.start()
    for copy in copies:
        copy.wait()
    core = lax.axis_index(lane) & 1
    for side in (1, 0):
        base = (core if side == 0 else 1 - core) * half_blocks
        for i in range(half_blocks):
            weight = scale[pl.ds(base + i, 1), :] * sw[sets[base + i]]
            weight = jnp.broadcast_to(weight, (width, width)).T
            rows = pl.ds(pl.multiple_of((base + i) * width, width), width)
            for n, cols in enumerate(chunks):
                for m, col in enumerate(cols):
                    block = green[rows, (col - low) * width : (col - low + 1) * width]
                    value = (block.astype(jnp.float32) * weight).astype(jnp.bfloat16)
                    keep = fp[first + col, base + i] != 0
                    to = slice(m * half + i * width, m * half + (i + 1) * width)
                    outs[2 * n + side][to, :] = jnp.where(keep, value, jnp.zeros_like(value))


def prep(chunks, lane, panel_index, footprint, set_index, set_weight, scale, green):
    rows = green.shape[0]
    width = rows // footprint.shape[1]
    count = sum(len(cols) for cols in chunks)
    shapes = [jax.ShapeDtypeStruct((rows // 2 * len(cols), width), jnp.bfloat16) for cols in chunks for _ in range(2)]
    return pl.pallas_call(
        functools.partial(prep_body, chunks, lane, width),
        in_specs=[smem()] + [pl.BlockSpec(memory_space=pltpu.HBM)] * 5,
        out_specs=[whole_vmem()] * len(shapes),
        out_shape=shapes,
        scratch_shapes=[
            pltpu.SMEM(footprint.shape, jnp.int32),
            pltpu.SMEM(set_index.shape, jnp.int32),
            pltpu.SMEM(set_weight.shape, jnp.float32),
            pltpu.VMEM(scale.shape, jnp.float32),
            pltpu.VMEM((rows, count * width), jnp.bfloat16),
            pltpu.SemaphoreType.DMA((5,)),
        ],
        compiler_params=pltpu.CompilerParams(vmem_limit_bytes=PREP_LIMIT),
        name="weigh_panel",
    )(panel_index, footprint, set_index, set_weight, scale, green)


def turn_body(blocks, width, step_blocks, fp_ref, green_ref, out_ref, done_ref):
    step = pl.program_id(0)
    done_ref[...] = jnp.zeros_like(done_ref)
    for i in range(step_blocks):
        for j in range(blocks):
            block = green_ref[i * width : (i + 1) * width, j * width : (j + 1) * width]
            keep = fp_ref[j, step * step_blocks + i] != 0
            block = jnp.where(keep, block, jnp.zeros_like(block))
            out_ref[j * width : (j + 1) * width, i * width : (i + 1) * width] = block.T


def turn(footprint, green):
    rows, cols = green.shape
    blocks, pblocks = footprint.shape
    width = rows // pblocks
    steps = 4
    return pl.pallas_call(
        functools.partial(turn_body, blocks, width, pblocks // steps),
        grid=(steps,),
        in_specs=[smem(), pl.BlockSpec((rows // steps, cols), lambda i: (i, 0))],
        out_specs=[pl.BlockSpec((cols, rows // steps), lambda i: (0, i)), pl.BlockSpec((8, width), lambda i: (0, 0))],
        out_shape=[jax.ShapeDtypeStruct((cols, rows), jnp.bfloat16), jax.ShapeDtypeStruct((8, width), jnp.bfloat16)],
        compiler_params=pltpu.CompilerParams(vmem_limit_bytes=VMEM_LIMIT),
        name="mask_and_turn",
    )(footprint, green)


def gram_body(shares, count, meta, turned_ref, *refs):
    pieces, outs, done_ref, total_ref = refs[:count], refs[count:-2], refs[-2], refs[-1]
    done_ref[...] = jnp.zeros_like(done_ref)
    core, group = meta[0], meta[1]
    half = turned_ref.shape[1] // 2
    share = turned_ref.shape[0] // shares

    def half_of(side):
        return pl.ds(pl.multiple_of((core if side == 0 else 1 - core) * half, half), half)

    def columns(side):
        some = pieces[side::2]
        return jnp.concatenate([p[c : c + half, :] for p in some for c in range(0, p.shape[0], half)], 1)

    @pl.loop(0, shares)
    def _(s):
        at = pl.ds(pl.multiple_of((group ^ s) * share, share), share)
        total_ref[pl.ds(pl.multiple_of(s * share, share), share), :] = sum(
            jnp.dot(turned_ref[at, half_of(side)], columns(side), preferred_element_type=jnp.float32)
            for side in range(2)
        )

    for s in range(shares):
        outs[s][...] = total_ref[s * share : (s + 1) * share, :].astype(outs[s].dtype)


def gram(shares, meta, turned, pieces):
    unknowns, pixels = turned.shape
    cols = sum(p.shape[0] for p in pieces[::2]) // (pixels // 2)
    share, wide = unknowns // shares, pieces[0].shape[1] * cols
    return pl.pallas_call(
        functools.partial(gram_body, shares, len(pieces)),
        in_specs=[smem()] + [whole_vmem()] * (1 + len(pieces)),
        out_specs=[whole_vmem()] * (shares + 1),
        out_shape=[jax.ShapeDtypeStruct((share, wide), jnp.float32 if s == 0 else jnp.bfloat16) for s in range(shares)]
        + [jax.ShapeDtypeStruct((8, pieces[0].shape[1]), jnp.bfloat16)],
        scratch_shapes=[pltpu.VMEM((unknowns, wide), jnp.float32)],
        compiler_params=pltpu.CompilerParams(vmem_limit_bytes=VMEM_LIMIT),
        name="partial_gram",
    )(meta, turned, *pieces)


def sum_body(shares, *refs):
    out_ref, parts = refs[-1], refs[:-1]
    at = 0
    for k in range(0, len(parts), shares):
        total = parts[k][...]
        for s in range(1, shares):
            total += parts[k + s][...].astype(jnp.float32)
        out_ref[:, at : at + total.shape[1]] = total
        at += total.shape[1]


def total_of(shares, parts, panel_cols):
    return pl.pallas_call(
        functools.partial(sum_body, shares),
        in_specs=[whole_vmem()] * len(parts),
        out_specs=whole_vmem(),
        out_shape=jax.ShapeDtypeStruct((parts[0].shape[0], panel_cols), jnp.float32),
        compiler_params=pltpu.CompilerParams(vmem_limit_bytes=VMEM_LIMIT),
        name="sum_groups",
    )(*parts)


def spread(owner, chips):
    levels = {}

    def serve(source, run, depth):
        if not run:
            return
        middle = run[len(run) // 2] if len(run) > 2 else run[0]
        levels.setdefault(depth, []).append((source, middle))
        at = run.index(middle)
        serve(middle, run[:at][::-1], depth + 1)
        serve(middle, run[at + 1 :], depth + 1)

    serve(owner, list(range(owner + 1, chips)), 0)
    serve(owner, list(range(owner - 1, -1, -1)), 0)
    rounds = []
    for depth in sorted(levels):
        left = levels[depth]
        while left:
            used, later, now = set(), [], []
            for edge in left:
                (later if edge[0] in used else now).append(edge)
                used.add(edge[0])
            rounds.append((depth, now))
            left = later
    return rounds


def after(value, *zeros):
    for zero in zeros:
        value = value + zero[:1]
    return value


def on_device(groups, lanes, green, footprint, set_index, set_weight, pixel_scale, panel_index):
    rows, cols = green.shape
    pblocks, blocks = footprint.shape
    width = rows // pblocks
    half = rows // 2
    chips = lanes // 2
    row = lax.axis_index("row")
    core, chip = row & 1, row >> 1
    meta = jnp.stack([core, lax.axis_index("grp")])
    owner = (panel_index[0] * PANEL) // blocks
    swap = [(r, r ^ 1) for r in range(lanes)]
    met = footprint.T
    small = ("row", panel_index, met, set_index, set_weight, pixel_scale.reshape(pblocks, width), green)
    chunks = CHUNKS if chips <= 4 else ((0, 1, 2, 3),)
    batches = BATCHES if len(chunks) == len(CHUNKS) else ((0,),)
    last = len(chunks) - 1

    own, other = prep(chunks[:1], *small)
    start = jnp.where(row == owner, own, lax.ppermute(other, "row", swap))
    rest = prep(chunks[1:], *small) if last else []

    def exchange(shares):
        return [shares[0]] + [
            lax.ppermute(shares[s], "grp", [(g, g ^ s) for g in range(groups)]) for s in range(1, groups)
        ]

    def from_chip(source):
        rounds = spread(source, chips)
        deepest = rounds[-1][0]
        parent = {b: n for n, (_, edges) in enumerate(rounds) for _, b in edges}

        def run(meta, met, green, start, *rest):
            sources = [start]
            for k in range(last):
                sources.append(jnp.where(row == owner, rest[2 * k], lax.ppermute(rest[2 * k + 1], "row", swap)))
            came, held, pieces, parts = {}, list(sources), {}, []
            turned, ready = turn(met, green)
            for step in range(len(chunks) + deepest):
                for n, (depth, edges) in enumerate(rounds):
                    k = step - depth
                    if not 0 <= k <= last:
                        continue
                    if depth == 0:
                        sent = sources[k]
                    else:
                        sent = came[parent[edges[0][0]], k]
                        for a, _ in edges[1:]:
                            sent = jnp.where(chip == a, came[parent[a], k], sent)
                        if k == 0 and depth == 1:
                            sent = after(sent, ready)
                    came[n, k] = lax.ppermute(sent, "row", [(2 * a + c, 2 * b + c) for a, b in edges for c in range(2)])
                    for _, b in edges:
                        held[k] = jnp.where(chip == b, came[n, k], held[k])
                k = step - deepest
                if k >= 0:
                    if k == last and parts:
                        held[k] = after(held[k], *ties)
                    pieces[k] = (held[k], lax.ppermute(held[k], "row", swap))
                    for batch in batches:
                        if k == batch[-1]:
                            shares = gram(groups, meta, turned, [p for b in batch for p in pieces[b]])
                            fresh = exchange(shares[:groups])
                            parts += fresh
                            if TIE == 0:
                                ties = []
                            elif TIE == 1:
                                ties = [shares[groups]]
                            else:
                                ties = [p[:8, :width] * jnp.bfloat16(0) for p in fresh[1:]]
            return total_of(groups, parts, PANEL * width)

        return run

    return lax.switch(owner >> 1, [from_chip(source) for source in range(chips)], meta, met, green, start, *rest)


def solution(mesh):
    in_specs = (P("grp", "row"), P("grp", "row"), P("grp"), P(), P("grp"), P())
    out_specs = P(("row", "grp"), None)
    body = functools.partial(on_device, mesh.shape["grp"], mesh.shape["row"])
    return jax.shard_map(body, mesh=mesh, in_specs=in_specs, out_specs=out_specs, check_vma=False)
```

```python
import functools
import jax
import jax.numpy as jnp
from jax import lax
from jax.experimental import pallas as pl
from jax.experimental.pallas import tpu as pltpu
from jax.sharding import PartitionSpec as P

PANEL = 4
CHUNKS = ((0,), (1,), (2,), (3,))
BATCHES = ((0, 1), (2, 3))
TIE = 1
MERGE = False
FULL = True
GATE = "held"
VMEM_LIMIT = 16 * 1024 * 1024
PREP_LIMIT = 60 * 1024 * 1024


def whole_vmem():
    return pl.BlockSpec(memory_space=pltpu.VMEM)


def smem():
    return pl.BlockSpec(memory_space=pltpu.SMEM)


def prep_body(chunks, lane, width, panel, fp_hbm, set_hbm, sw_hbm, scale_hbm, green_hbm, *refs):
    outs, (fp, sets, sw, scale, green, sems) = refs[: 2 * len(chunks)], refs[2 * len(chunks) :]
    blocks, pblocks = fp_hbm.shape
    half_blocks = pblocks // 2
    half = half_blocks * width
    low = chunks[0][0]
    first = lax.rem(panel[0] * PANEL, blocks)
    at = pl.ds(pl.multiple_of((first + low) * width, width), green.shape[1])
    copies = [
        pltpu.make_async_copy(source, target, sems.at[n])
        for n, (source, target) in enumerate(
            ((fp_hbm, fp), (set_hbm, sets), (sw_hbm, sw), (scale_hbm, scale), (green_hbm.at[:, at], green))
        )
    ]
    for copy in copies:
        copy.start()
    for copy in copies:
        copy.wait()
    core = lax.axis_index(lane) & 1
    for side in (1, 0):
        base = (core if side == 0 else 1 - core) * half_blocks
        for i in range(half_blocks):
            weight = scale[pl.ds(base + i, 1), :] * sw[sets[base + i]]
            weight = jnp.broadcast_to(weight, (width, width)).T
            rows = pl.ds(pl.multiple_of((base + i) * width, width), width)
            for n, cols in enumerate(chunks):
                for m, col in enumerate(cols):
                    block = green[rows, (col - low) * width : (col - low + 1) * width]
                    value = (block.astype(jnp.float32) * weight).astype(jnp.bfloat16)
                    keep = fp[first + col, base + i] != 0
                    to = slice(m * half + i * width, m * half + (i + 1) * width)
                    outs[2 * n + side][to, :] = jnp.where(keep, value, jnp.zeros_like(value))


def prep(chunks, lane, panel_index, footprint, set_index, set_weight, scale, green):
    rows = green.shape[0]
    width = rows // footprint.shape[1]
    count = sum(len(cols) for cols in chunks)
    shapes = [jax.ShapeDtypeStruct((rows // 2 * len(cols), width), jnp.bfloat16) for cols in chunks for _ in range(2)]
    return pl.pallas_call(
        functools.partial(prep_body, chunks, lane, width),
        in_specs=[smem()] + [pl.BlockSpec(memory_space=pltpu.HBM)] * 5,
        out_specs=[whole_vmem()] * len(shapes),
        out_shape=shapes,
        scratch_shapes=[
            pltpu.SMEM(footprint.shape, jnp.int32),
            pltpu.SMEM(set_index.shape, jnp.int32),
            pltpu.SMEM(set_weight.shape, jnp.float32),
            pltpu.VMEM(scale.shape, jnp.float32),
            pltpu.VMEM((rows, count * width), jnp.bfloat16),
            pltpu.SemaphoreType.DMA((5,)),
        ],
        compiler_params=pltpu.CompilerParams(vmem_limit_bytes=PREP_LIMIT),
        name="weigh_panel",
    )(panel_index, footprint, set_index, set_weight, scale, green)


def gram_body(shares, count, width, meta, fp_ref, green_ref, *refs):
    pieces, outs, done_ref = refs[:count], refs[count:-4], refs[-4]
    total_ref, masked_ref, left_ref = refs[-3:]
    done_ref[...] = jnp.zeros_like(done_ref)
    core, group = meta[0], meta[1]
    rows, cols = green_ref.shape
    half = rows // 2
    share = cols // shares
    step = masked_ref.shape[1]
    for side in range(2):
        to = pl.ds(pl.multiple_of((core if side == 0 else 1 - core) * half, half), half)
        some = [p[c : c + half, :] for p in pieces[side::2] for c in range(0, p.shape[0], half)]
        for n, piece in enumerate(some):
            left_ref[n * width : (n + 1) * width, to] = piece.T

    @pl.loop(0, cols // step)
    def _(n):
        for i in range(rows // width):
            for j in range(step // width):
                at = pl.ds(pl.multiple_of(n * step + j * width, width), width)
                block = green_ref[i * width : (i + 1) * width, at]
                block = jnp.where(fp_ref[n * (step // width) + j, i] != 0, block, jnp.zeros_like(block))
                masked_ref[i * width : (i + 1) * width, j * width : (j + 1) * width] = block
        total = jnp.dot(left_ref[...], masked_ref[...], preferred_element_type=jnp.float32)
        total_ref[pl.ds(pl.multiple_of(n * step, step), step), :] = total.T

    for s in range(shares):
        at = pl.ds(pl.multiple_of((group ^ s) * share, share), share)
        outs[s][...] = total_ref[at, :].astype(outs[s].dtype)


def gram(shares, meta, footprint, green, pieces):
    rows, unknowns = green.shape
    width = rows // footprint.shape[1]
    share, wide = unknowns // shares, sum(p.shape[0] for p in pieces[::2]) // (rows // 2) * width
    return pl.pallas_call(
        functools.partial(gram_body, shares, len(pieces), width),
        in_specs=[smem()] * 2 + [whole_vmem()] * (1 + len(pieces)),
        out_specs=[whole_vmem()] * (shares + 1),
        out_shape=[jax.ShapeDtypeStruct((share, wide), jnp.float32 if s == 0 else jnp.bfloat16) for s in range(shares)]
        + [jax.ShapeDtypeStruct((8, width), jnp.bfloat16)],
        scratch_shapes=[
            pltpu.VMEM((unknowns, wide), jnp.float32),
            pltpu.VMEM((rows, 2 * width), jnp.bfloat16),
            pltpu.VMEM((wide, rows), jnp.bfloat16),
        ],
        compiler_params=pltpu.CompilerParams(vmem_limit_bytes=VMEM_LIMIT),
        name="partial_gram",
    )(meta, footprint, green, *pieces)


def sum_body(shares, *refs):
    out_ref, parts = refs[-1], refs[:-1]
    at = 0
    for k in range(0, len(parts), shares):
        total = parts[k][...]
        for s in range(1, shares):
            total += parts[k + s][...].astype(jnp.float32)
        out_ref[:, at : at + total.shape[1]] = total
        at += total.shape[1]


def total_of(shares, parts, panel_cols):
    return pl.pallas_call(
        functools.partial(sum_body, shares),
        in_specs=[whole_vmem()] * len(parts),
        out_specs=whole_vmem(),
        out_shape=jax.ShapeDtypeStruct((parts[0].shape[0], panel_cols), jnp.float32),
        compiler_params=pltpu.CompilerParams(vmem_limit_bytes=VMEM_LIMIT),
        name="sum_groups",
    )(*parts)


def spread(owner, chips):
    levels = {}

    def serve(source, run, depth):
        if not run:
            return
        middle = run[len(run) // 2] if len(run) > 2 else run[0]
        levels.setdefault(depth, []).append((source, middle))
        at = run.index(middle)
        serve(middle, run[:at][::-1], depth + 1)
        serve(middle, run[at + 1 :], depth + 1)

    serve(owner, list(range(owner + 1, chips)), 0)
    serve(owner, list(range(owner - 1, -1, -1)), 0)
    rounds = []
    for depth in sorted(levels):
        left = levels[depth]
        while left:
            used, later, now = set(), [], []
            for edge in left:
                (later if edge[0] in used else now).append(edge)
                used.add(edge[0])
            rounds.append((depth, now))
            left = later
    return rounds


def links(edge):
    a, b = edge
    return {(c, c + 1) for c in range(a, b)} | {(c + 1, c) for c in range(b, a)}


def pairs(edges, rounds, first):
    forth = [(2 * a + c, 2 * b + c) for a, b in edges for c in range(2)]
    taken = set().union(*(links(e) for _, some in rounds for e in some))
    back = set().union(*(links((b, a)) for a, b in edges))
    busy = [c for e in edges for c in e]
    if not FULL or len(set(busy)) < len(busy) or (back & taken and not first):
        return forth
    lanes = 2 * (1 + max(c for _, some in rounds for e in some for c in e))
    rest = [(r, r ^ 1) for r in range(lanes) if r >> 1 not in busy]
    return forth + [(b, a) for a, b in forth] + rest


def after(value, *zeros):
    for zero in zeros:
        value = value + zero[:1]
    return value


def on_device(groups, lanes, green, footprint, set_index, set_weight, pixel_scale, panel_index):
    rows, cols = green.shape
    pblocks, blocks = footprint.shape
    width = rows // pblocks
    half = rows // 2
    chips = lanes // 2
    row = lax.axis_index("row")
    core, chip = row & 1, row >> 1
    meta = jnp.stack([core, lax.axis_index("grp")])
    owner = (panel_index[0] * PANEL) // blocks
    swap = [(r, r ^ 1) for r in range(lanes)]
    met = footprint.T
    small = ("row", panel_index, met, set_index, set_weight, pixel_scale.reshape(pblocks, width), green)
    chunks = CHUNKS if chips <= 4 else ((0, 1, 2, 3),)
    batches = BATCHES if len(chunks) == len(CHUNKS) else ((0,),)
    last = len(chunks) - 1

    own, other = prep(chunks[:1], *small)
    start = jnp.where(row == owner, own, lax.ppermute(other, "row", swap))
    rest = prep((sum(chunks[1:], ()),) if MERGE else chunks[1:], *small) if last else []

    def exchange(shares):
        return [shares[0]] + [
            lax.ppermute(shares[s], "grp", [(g, g ^ s) for g in range(groups)]) for s in range(1, groups)
        ]

    def from_chip(source):
        rounds = spread(source, chips)
        deepest = rounds[-1][0]
        parent = {b: n for n, (_, edges) in enumerate(rounds) for _, b in edges}

        def run(meta, met, green, start, *rest):
            sources = [start]
            if rest and MERGE:
                own, other = rest[0], lax.ppermute(rest[1], "row", swap)
                for k in range(last):
                    at = slice(k * half, (k + 1) * half)
                    sources.append(jnp.where(row == owner, own[at], other[at]))
            elif rest:
                for k in range(last):
                    sources.append(jnp.where(row == owner, rest[2 * k], lax.ppermute(rest[2 * k + 1], "row", swap)))
            came, held, pieces, parts = {}, list(sources), {}, []
            for step in range(len(chunks) + deepest):
                for n, (depth, edges) in enumerate(rounds):
                    k = step - depth
                    if not 0 <= k <= last:
                        continue
                    if depth == 0:
                        sent = sources[k]
                    else:
                        sent = came[parent[edges[0][0]], k]
                        for a, _ in edges[1:]:
                            sent = jnp.where(chip == a, came[parent[a], k], sent)
                    if GATE == "sent" and k == last and depth and parts:
                        sent = after(sent, *ties)
                    came[n, k] = lax.ppermute(sent, "row", pairs(edges, rounds, depth == 0 and k == 0))
                    for _, b in edges:
                        held[k] = jnp.where(chip == b, came[n, k], held[k])
                k = step - deepest
                if k >= 0:
                    if GATE == "held" and k == last and parts:
                        held[k] = after(held[k], *ties)
                    pieces[k] = (held[k], lax.ppermute(held[k], "row", swap))
                    for batch in batches:
                        if k == batch[-1]:
                            shares = gram(groups, meta, met, green, [p for b in batch for p in pieces[b]])
                            fresh = exchange(shares[:groups])
                            parts += fresh
                            if TIE == 0:
                                ties = []
                            elif TIE == 1:
                                ties = [shares[groups]]
                            elif TIE == 3:
                                ties = [fresh[1][:8, :width] * jnp.bfloat16(0)]
                            else:
                                ties = [p[:8, :width] * jnp.bfloat16(0) for p in fresh[1:]]
            return total_of(groups, parts, PANEL * width)

        return run

    return lax.switch(owner >> 1, [from_chip(source) for source in range(chips)], meta, met, green, start, *rest)


def solution(mesh):
    in_specs = (P("grp", "row"), P("grp", "row"), P("grp"), P(), P("grp"), P())
    out_specs = P(("row", "grp"), None)
    body = functools.partial(on_device, mesh.shape["grp"], mesh.shape["row"])
    return jax.shard_map(body, mesh=mesh, in_specs=in_specs, out_specs=out_specs, check_vma=False)
```

```python
import functools
import jax
import jax.numpy as jnp
from jax import lax
from jax.experimental import pallas as pl
from jax.experimental.pallas import tpu as pltpu
from jax.sharding import PartitionSpec as P

PANEL = 4
CHUNKS = ((0,), (1,), (2,), (3,))
BATCHES = ((0, 1), (2, 3))
GATES = ((3, ((1, 0),)),)
MERGE = False
STEP = 4
SWAPPED = True
FULL = True
VMEM_LIMIT = 16 * 1024 * 1024
PREP_LIMIT = 60 * 1024 * 1024


def whole_vmem():
    return pl.BlockSpec(memory_space=pltpu.VMEM)


def smem():
    return pl.BlockSpec(memory_space=pltpu.SMEM)


def prep_body(chunks, lane, width, panel, fp_hbm, set_hbm, sw_hbm, scale_hbm, green_hbm, *refs):
    outs, (fp, sets, sw, scale, green, sems) = refs[: 2 * len(chunks)], refs[2 * len(chunks) :]
    blocks, pblocks = fp_hbm.shape
    half_blocks = pblocks // 2
    low = chunks[0][0]
    first = lax.rem(panel[0] * PANEL, blocks)
    at = pl.ds(pl.multiple_of((first + low) * width, width), green.shape[1])
    copies = [
        pltpu.make_async_copy(source, target, sems.at[n])
        for n, (source, target) in enumerate(
            ((fp_hbm, fp), (set_hbm, sets), (sw_hbm, sw), (scale_hbm, scale), (green_hbm.at[:, at], green))
        )
    ]
    for copy in copies:
        copy.start()
    for copy in copies:
        copy.wait()
    core = lax.axis_index(lane) & 1
    for side in (1, 0):
        base = (core if side == 0 else 1 - core) * half_blocks
        for i in range(half_blocks):
            weight = scale[pl.ds(base + i, 1), :] * sw[sets[base + i]]
            rows = pl.ds(pl.multiple_of((base + i) * width, width), width)
            for n, cols in enumerate(chunks):
                for m, col in enumerate(cols):
                    block = green[rows, (col - low) * width : (col - low + 1) * width]
                    value = (block.T.astype(jnp.float32) * weight).astype(jnp.bfloat16)
                    keep = fp[first + col, base + i] != 0
                    to = (slice(m * width, (m + 1) * width), slice(i * width, (i + 1) * width))
                    outs[2 * n + side][to] = jnp.where(keep, value, jnp.zeros_like(value))


def prep(chunks, lane, panel_index, footprint, set_index, set_weight, scale, green):
    rows = green.shape[0]
    width = rows // footprint.shape[1]
    count = sum(len(cols) for cols in chunks)
    shapes = [jax.ShapeDtypeStruct((len(cols) * width, rows // 2), jnp.bfloat16) for cols in chunks for _ in range(2)]
    return pl.pallas_call(
        functools.partial(prep_body, chunks, lane, width),
        in_specs=[smem()] + [pl.BlockSpec(memory_space=pltpu.HBM)] * 5,
        out_specs=[whole_vmem()] * len(shapes),
        out_shape=shapes,
        scratch_shapes=[
            pltpu.SMEM(footprint.shape, jnp.int32),
            pltpu.SMEM(set_index.shape, jnp.int32),
            pltpu.SMEM(set_weight.shape, jnp.float32),
            pltpu.VMEM(scale.shape, jnp.float32),
            pltpu.VMEM((rows, count * width), jnp.bfloat16),
            pltpu.SemaphoreType.DMA((5,)),
        ],
        compiler_params=pltpu.CompilerParams(vmem_limit_bytes=PREP_LIMIT),
        name="weigh_panel",
    )(panel_index, footprint, set_index, set_weight, scale, green)


def gram_body(shares, count, width, meta, fp_ref, green_ref, *refs):
    pieces, outs, done_ref, total_ref, masked_ref = refs[:count], refs[count:-3], refs[-3], refs[-2], refs[-1]
    done_ref[...] = jnp.zeros_like(done_ref)
    core, group = meta[0], meta[1]
    rows, cols = green_ref.shape
    half = rows // 2
    step = masked_ref.shape[1]

    @pl.loop(0, cols // step)
    def _(n):
        for i in range(rows // width):
            for j in range(step // width):
                at = pl.ds(pl.multiple_of(n * step + j * width, width), width)
                block = green_ref[i * width : (i + 1) * width, at]
                block = jnp.where(fp_ref[n * (step // width) + j, i] != 0, block, jnp.zeros_like(block))
                masked_ref[i * width : (i + 1) * width, j * width : (j + 1) * width] = block
        total = 0.0
        for side in range(2):
            at = pl.ds(pl.multiple_of((core if side == 0 else 1 - core) * half, half), half)
            left = jnp.concatenate([p[...] for p in pieces[side::2]], 0)
            total += jnp.dot(left, masked_ref[at, :], preferred_element_type=jnp.float32)
        total_ref[:, pl.ds(pl.multiple_of(n * step, step), step)] = total

    share = cols // shares
    for s in range(len(outs)):
        if len(outs) > 1:
            outs[s][...] = total_ref[:, pl.ds(pl.multiple_of((group ^ s) * share, share), share)].astype(outs[s].dtype)
        else:
            outs[s][...] = total_ref[...]


def gram(shares, meta, footprint, green, pieces):
    rows, unknowns = green.shape
    width = rows // footprint.shape[1]
    share, wide = unknowns // shares, sum(p.shape[0] for p in pieces[::2])
    apart = share % width == 0
    shapes = [jax.ShapeDtypeStruct((wide, share), jnp.float32 if s == 0 else jnp.bfloat16) for s in range(shares)]
    out = pl.pallas_call(
        functools.partial(gram_body, shares, len(pieces), width),
        in_specs=[smem()] * 2 + [whole_vmem()] * (1 + len(pieces)),
        out_specs=[whole_vmem()] * ((shares if apart else 1) + 1),
        out_shape=(shapes if apart else [jax.ShapeDtypeStruct((wide, unknowns), jnp.float32)])
        + [jax.ShapeDtypeStruct((8, rows // 2), jnp.bfloat16)],
        scratch_shapes=[pltpu.VMEM((wide, unknowns), jnp.float32), pltpu.VMEM((rows, STEP * width), jnp.bfloat16)],
        compiler_params=pltpu.CompilerParams(vmem_limit_bytes=VMEM_LIMIT),
        name="partial_gram",
    )(meta, footprint, green, *pieces)
    if apart:
        return out
    cut = [lax.dynamic_slice_in_dim(out[0], (meta[1] ^ s) * share, share, 1).astype(shapes[s].dtype) for s in range(shares)]
    return [*cut, out[1]]


def sum_body(shares, *refs):
    out_ref, parts = refs[-1], refs[:-1]
    at = 0
    for k in range(0, len(parts), shares):
        total = parts[k][...]
        for s in range(1, shares):
            total += parts[k + s][...].astype(jnp.float32)
        out_ref[:, at : at + total.shape[0]] = total.T
        at += total.shape[0]


def total_of(shares, parts, panel_cols):
    share = parts[0].shape[1]
    if share % 128:
        return jnp.concatenate([sum(p.astype(jnp.float32) for p in parts[k : k + shares]) for k in range(0, len(parts), shares)]).T
    return pl.pallas_call(
        functools.partial(sum_body, shares),
        in_specs=[whole_vmem()] * len(parts),
        out_specs=whole_vmem(),
        out_shape=jax.ShapeDtypeStruct((share, panel_cols), jnp.float32),
        compiler_params=pltpu.CompilerParams(vmem_limit_bytes=VMEM_LIMIT),
        name="sum_groups",
    )(*parts)


def spread(owner, chips):
    levels = {}

    def serve(source, run, depth):
        if not run:
            return
        middle = run[len(run) // 2] if len(run) > 2 else run[0]
        levels.setdefault(depth, []).append((source, middle))
        at = run.index(middle)
        serve(middle, run[:at][::-1], depth + 1)
        serve(middle, run[at + 1 :], depth + 1)

    serve(owner, list(range(owner + 1, chips)), 0)
    serve(owner, list(range(owner - 1, -1, -1)), 0)
    rounds = []
    for depth in sorted(levels):
        left = levels[depth]
        while left:
            used, later, now = set(), [], []
            for edge in left:
                (later if edge[0] in used else now).append(edge)
                used.add(edge[0])
            rounds.append((depth, now))
            left = later
    return rounds


def links(edge):
    a, b = edge
    return {(c, c + 1) for c in range(a, b)} | {(c + 1, c) for c in range(b, a)}


def pairs(edges, rounds, first):
    forth = [(2 * a + c, 2 * b + c) for a, b in edges for c in range(2)]
    taken = set().union(*(links(e) for _, some in rounds for e in some))
    back = set().union(*(links((b, a)) for a, b in edges))
    busy = [c for e in edges for c in e]
    if not FULL or len(set(busy)) < len(busy) or (back & taken and not first):
        return forth
    lanes = 2 * (1 + max(c for _, some in rounds for e in some for c in e))
    rest = [(r, r ^ 1) for r in range(lanes) if r >> 1 not in busy]
    return forth + [(b, a) for a, b in forth] + rest


def after(value, *zeros):
    for zero in zeros:
        value = value + zero[:1]
    return value


def on_device(groups, lanes, green, footprint, set_index, set_weight, pixel_scale, panel_index):
    rows, cols = green.shape
    pblocks, blocks = footprint.shape
    width = rows // pblocks
    half = rows // 2
    chips = lanes // 2
    row = lax.axis_index("row")
    core, chip = row & 1, row >> 1
    meta = jnp.stack([core, lax.axis_index("grp")])
    owner = (panel_index[0] * PANEL) // blocks
    swap = [(r, r ^ 1) for r in range(lanes)]
    met = footprint.T
    small = ("row", panel_index, met, set_index, set_weight, pixel_scale.reshape(pblocks, width), green)
    chunks = CHUNKS if chips <= 4 else ((0, 1, 2, 3),)
    batches = BATCHES if len(chunks) == len(CHUNKS) else ((0,),)
    last = len(chunks) - 1

    own, other = prep(chunks[:1], *small)
    start = jnp.where(row == owner, own, lax.ppermute(other, "row", swap))
    rest = prep((sum(chunks[1:], ()),) if MERGE else chunks[1:], *small) if last else []

    def exchange(shares):
        return [shares[0]] + [
            lax.ppermute(shares[s], "grp", [(g, g ^ s) for g in range(groups)]) for s in range(1, groups)
        ]

    def from_chip(source):
        rounds = spread(source, chips)
        if SWAPPED and len(rounds) == 3 and rounds[1][0] == rounds[2][0]:
            rounds = [rounds[0], rounds[2], rounds[1]]
        deepest = rounds[-1][0]
        parent = {b: n for n, (_, edges) in enumerate(rounds) for _, b in edges}

        def run(meta, met, green, start, *rest):
            sources = [start]
            if rest and MERGE:
                own, other = rest[0], lax.ppermute(rest[1], "row", swap)
                for k in range(last):
                    at = slice(k * width, (k + 1) * width)
                    sources.append(jnp.where(row == owner, own[at], other[at]))
            elif rest:
                for k in range(last):
                    sources.append(jnp.where(row == owner, rest[2 * k], lax.ppermute(rest[2 * k + 1], "row", swap)))
            came, held, pieces, parts, signs = {}, list(sources), {}, [], {}
            gates = {k: (lambda some=some: [signs[b][n] for b, n in some]) for k, some in GATES} if last else {}
            for step in range(len(chunks) + deepest):
                for n, (depth, edges) in enumerate(rounds):
                    k = step - depth
                    if not 0 <= k <= last:
                        continue
                    if depth == 0:
                        sent = sources[k]
                    else:
                        sent = came[parent[edges[0][0]], k]
                        for a, _ in edges[1:]:
                            sent = jnp.where(chip == a, came[parent[a], k], sent)
                    came[n, k] = lax.ppermute(sent, "row", pairs(edges, rounds, depth == 0 and k == 0))
                    for _, b in edges:
                        held[k] = jnp.where(chip == b, came[n, k], held[k])
                k = step - deepest
                if k >= 0:
                    if k in gates:
                        held[k] = after(held[k], *gates[k]())
                    pieces[k] = (held[k], lax.ppermute(held[k], "row", swap))
                    for batch in batches:
                        if k == batch[-1]:
                            shares = gram(groups, meta, met, green, [p for b in batch for p in pieces[b]])
                            fresh = exchange(shares[:groups])
                            parts += fresh
                            signs[k] = (shares[groups], *(p[:1, :1] * jnp.bfloat16(0) for p in fresh[1:]))
            return total_of(groups, parts, PANEL * width)

        return run

    return lax.switch(owner >> 1, [from_chip(source) for source in range(chips)], meta, met, green, start, *rest)


def solution(mesh):
    in_specs = (P("grp", "row"), P("grp", "row"), P("grp"), P(), P("grp"), P())
    out_specs = P(("row", "grp"), None)
    body = functools.partial(on_device, mesh.shape["grp"], mesh.shape["row"])
    return jax.shard_map(body, mesh=mesh, in_specs=in_specs, out_specs=out_specs, check_vma=False)
```

```python
import functools
import jax
import jax.numpy as jnp
from jax import lax
from jax.experimental import pallas as pl
from jax.experimental.pallas import tpu as pltpu
from jax.sharding import PartitionSpec as P

PANEL = 4
CHUNKS = ((0,), (1,), (2,), (3,))
BATCHES = ((0, 1), (2, 3))
ALLPREP = False
STEP = 4
SWAPPED = True
FULL = True
VMEM_LIMIT = 16 * 1024 * 1024
PREP_LIMIT = 60 * 1024 * 1024


def whole_vmem():
    return pl.BlockSpec(memory_space=pltpu.VMEM)


def smem():
    return pl.BlockSpec(memory_space=pltpu.SMEM)


def prep_body(chunks, lane, width, panel, fp_hbm, set_hbm, sw_hbm, scale_hbm, green_hbm, *refs):
    outs, (fp, sets, sw, scale, green, sems) = refs[: 2 * len(chunks)], refs[2 * len(chunks) :]
    blocks, pblocks = fp_hbm.shape
    half_blocks = pblocks // 2
    low = chunks[0][0]
    first = lax.rem(panel[0] * PANEL, blocks)
    at = pl.ds(pl.multiple_of((first + low) * width, width), green.shape[1])
    copies = [
        pltpu.make_async_copy(source, target, sems.at[n])
        for n, (source, target) in enumerate(
            ((fp_hbm, fp), (set_hbm, sets), (sw_hbm, sw), (scale_hbm, scale), (green_hbm.at[:, at], green))
        )
    ]
    mine = lax.axis_index(lane) == panel[0] * PANEL // blocks

    @pl.when(mine)
    def _():
        for copy in copies:
            copy.start()
        for copy in copies:
            copy.wait()
        core = lax.axis_index(lane) & 1
        for side in (1, 0):
            base = (core if side == 0 else 1 - core) * half_blocks
            for i in range(half_blocks):
                weight = scale[pl.ds(base + i, 1), :] * sw[sets[base + i]]
                rows = pl.ds(pl.multiple_of((base + i) * width, width), width)
                for n, cols in enumerate(chunks):
                    for m, col in enumerate(cols):
                        block = green[rows, (col - low) * width : (col - low + 1) * width]
                        value = (block.T.astype(jnp.float32) * weight).astype(jnp.bfloat16)
                        keep = fp[first + col, base + i] != 0
                        to = (slice(m * width, (m + 1) * width), slice(i * width, (i + 1) * width))
                        outs[2 * n + side][to] = jnp.where(keep, value, jnp.zeros_like(value))

    @pl.when(jnp.logical_not(mine))
    def _():
        for out in outs:
            out[...] = jnp.zeros_like(out)


def prep(chunks, lane, panel_index, footprint, set_index, set_weight, scale, green):
    rows = green.shape[0]
    width = rows // footprint.shape[1]
    count = sum(len(cols) for cols in chunks)
    shapes = [jax.ShapeDtypeStruct((len(cols) * width, rows // 2), jnp.bfloat16) for cols in chunks for _ in range(2)]
    return pl.pallas_call(
        functools.partial(prep_body, chunks, lane, width),
        in_specs=[smem()] + [pl.BlockSpec(memory_space=pltpu.HBM)] * 5,
        out_specs=[whole_vmem()] * len(shapes),
        out_shape=shapes,
        scratch_shapes=[
            pltpu.SMEM(footprint.shape, jnp.int32),
            pltpu.SMEM(set_index.shape, jnp.int32),
            pltpu.SMEM(set_weight.shape, jnp.float32),
            pltpu.VMEM(scale.shape, jnp.float32),
            pltpu.VMEM((rows, count * width), jnp.bfloat16),
            pltpu.SemaphoreType.DMA((5,)),
        ],
        compiler_params=pltpu.CompilerParams(vmem_limit_bytes=PREP_LIMIT),
        name="weigh_panel",
    )(panel_index, footprint, set_index, set_weight, scale, green)


def gram_body(shares, count, width, fresh, meta, fp_ref, green_ref, *refs):
    pieces, outs, total_ref = refs[:count], refs[count:-1], refs[-1]
    core, group = meta[0], meta[1]
    rows, cols = green_ref.shape
    half = rows // 2
    step = STEP * width
    masked_ref = green_ref
    if fresh:
        outs, done_ref, masked_ref = outs[:-2], outs[-2], outs[-1]
        done_ref[...] = jnp.zeros_like(done_ref)

    @pl.loop(0, cols // step)
    def _(n):
        here = pl.ds(pl.multiple_of(n * step, step), step)
        if fresh:
            for i in range(rows // width):
                for j in range(step // width):
                    at = (slice(i * width, (i + 1) * width), pl.ds(pl.multiple_of(n * step + j * width, width), width))
                    block = green_ref[at]
                    masked_ref[at] = jnp.where(fp_ref[n * (step // width) + j, i] != 0, block, jnp.zeros_like(block))
        total = 0.0
        for side in range(2):
            at = pl.ds(pl.multiple_of((core if side == 0 else 1 - core) * half, half), half)
            left = jnp.concatenate([p[...] for p in pieces[side::2]], 0)
            total += jnp.dot(left, masked_ref[at, here], preferred_element_type=jnp.float32)
        total_ref[:, here] = total

    share = cols // shares
    for s in range(len(outs)):
        if len(outs) > 1:
            outs[s][...] = total_ref[:, pl.ds(pl.multiple_of((group ^ s) * share, share), share)].astype(outs[s].dtype)
        else:
            outs[s][...] = total_ref[...]


def gram(shares, meta, footprint, green, pieces, fresh):
    rows, unknowns = green.shape
    width = rows // footprint.shape[1]
    share, wide = unknowns // shares, sum(p.shape[0] for p in pieces[::2])
    apart = share % width == 0
    shapes = [jax.ShapeDtypeStruct((wide, share), jnp.float32 if s == 0 else jnp.bfloat16) for s in range(shares)]
    extra = [jax.ShapeDtypeStruct((8, rows // 2), jnp.bfloat16), jax.ShapeDtypeStruct(green.shape, green.dtype)]
    all_shapes = (shapes if apart else [jax.ShapeDtypeStruct((wide, unknowns), jnp.float32)]) + (extra if fresh else [])
    out = pl.pallas_call(
        functools.partial(gram_body, shares, len(pieces), width, fresh),
        in_specs=[smem()] * 2 + [whole_vmem()] * (1 + len(pieces)),
        out_specs=[whole_vmem()] * len(all_shapes),
        out_shape=all_shapes,
        scratch_shapes=[pltpu.VMEM((wide, unknowns), jnp.float32)],
        compiler_params=pltpu.CompilerParams(vmem_limit_bytes=VMEM_LIMIT),
        name="partial_gram",
    )(meta, footprint, green, *pieces)
    count = shares if apart else 1
    parts, rest = out[:count], out[count:]
    if not apart:
        parts = [
            lax.dynamic_slice_in_dim(out[0], (meta[1] ^ s) * share, share, 1).astype(shapes[s].dtype) for s in range(shares)
        ]
    return list(parts), rest


def sum_body(shares, *refs):
    out_ref, parts = refs[-1], refs[:-1]
    at = 0
    for k in range(0, len(parts), shares):
        total = parts[k][...]
        for s in range(1, shares):
            total += parts[k + s][...].astype(jnp.float32)
        out_ref[:, at : at + total.shape[0]] = total.T
        at += total.shape[0]


def total_of(shares, parts, panel_cols):
    share = parts[0].shape[1]
    if share % 128:
        return jnp.concatenate([sum(p.astype(jnp.float32) for p in parts[k : k + shares]) for k in range(0, len(parts), shares)]).T
    return pl.pallas_call(
        functools.partial(sum_body, shares),
        in_specs=[whole_vmem()] * len(parts),
        out_specs=whole_vmem(),
        out_shape=jax.ShapeDtypeStruct((share, panel_cols), jnp.float32),
        compiler_params=pltpu.CompilerParams(vmem_limit_bytes=VMEM_LIMIT),
        name="sum_groups",
    )(*parts)


def spread(owner, chips):
    levels = {}

    def serve(source, run, depth):
        if not run:
            return
        middle = run[len(run) // 2] if len(run) > 2 else run[0]
        levels.setdefault(depth, []).append((source, middle))
        at = run.index(middle)
        serve(middle, run[:at][::-1], depth + 1)
        serve(middle, run[at + 1 :], depth + 1)

    serve(owner, list(range(owner + 1, chips)), 0)
    serve(owner, list(range(owner - 1, -1, -1)), 0)
    rounds = []
    for depth in sorted(levels):
        left = levels[depth]
        while left:
            used, later, now = set(), [], []
            for edge in left:
                (later if edge[0] in used else now).append(edge)
                used.add(edge[0])
            rounds.append((depth, now))
            left = later
    return rounds


def links(edge):
    a, b = edge
    return {(c, c + 1) for c in range(a, b)} | {(c + 1, c) for c in range(b, a)}


def pairs(edges, rounds, first):
    forth = [(2 * a + c, 2 * b + c) for a, b in edges for c in range(2)]
    taken = set().union(*(links(e) for _, some in rounds for e in some))
    back = set().union(*(links((b, a)) for a, b in edges))
    busy = [c for e in edges for c in e]
    if not FULL or len(set(busy)) < len(busy) or (back & taken and not first):
        return forth
    lanes = 2 * (1 + max(c for _, some in rounds for e in some for c in e))
    rest = [(r, r ^ 1) for r in range(lanes) if r >> 1 not in busy]
    return forth + [(b, a) for a, b in forth] + rest


def after(value, *zeros):
    for zero in zeros:
        value = value + zero[:1]
    return value


def on_device(groups, lanes, green, footprint, set_index, set_weight, pixel_scale, panel_index):
    rows, cols = green.shape
    pblocks, blocks = footprint.shape
    width = rows // pblocks
    half = rows // 2
    chips = lanes // 2
    row = lax.axis_index("row")
    core, chip = row & 1, row >> 1
    meta = jnp.stack([core, lax.axis_index("grp")])
    owner = (panel_index[0] * PANEL) // blocks
    swap = [(r, r ^ 1) for r in range(lanes)]
    met = footprint.T
    small = ("row", panel_index, met, set_index, set_weight, pixel_scale.reshape(pblocks, width), green)
    chunks = CHUNKS if chips <= 4 else ((0, 1, 2, 3),)
    batches = BATCHES if len(chunks) == len(CHUNKS) else ((0,),)
    last = len(chunks) - 1

    weighed = prep(chunks, *small) if ALLPREP else prep(chunks[:1], *small)
    own, other = weighed[:2]
    start = jnp.where(row == owner, own, lax.ppermute(other, "row", swap))
    rest = weighed[2:] if ALLPREP else prep(chunks[1:], *small) if last else []

    def exchange(shares):
        return [shares[0]] + [
            lax.ppermute(shares[s], "grp", [(g, g ^ s) for g in range(groups)]) for s in range(1, groups)
        ]

    def from_chip(source):
        rounds = spread(source, chips)
        if SWAPPED and len(rounds) == 3 and rounds[1][0] == rounds[2][0]:
            rounds = [rounds[0], rounds[2], rounds[1]]
        deepest = rounds[-1][0]
        parent = {b: n for n, (_, edges) in enumerate(rounds) for _, b in edges}

        def run(meta, met, green, start, *rest):
            sources = [start]
            for k in range(last):
                sources.append(jnp.where(row == owner, rest[2 * k], lax.ppermute(rest[2 * k + 1], "row", swap)))
            came, held, pieces, parts = {}, list(sources), {}, []
            done, values = None, green
            for step in range(len(chunks) + deepest):
                for n, (depth, edges) in reversed(list(enumerate(rounds))):
                    k = step - depth
                    if not 0 <= k <= last:
                        continue
                    if depth == 0:
                        sent = sources[k]
                    else:
                        sent = came[parent[edges[0][0]], k]
                        for a, _ in edges[1:]:
                            sent = jnp.where(chip == a, came[parent[a], k], sent)
                    came[n, k] = lax.ppermute(sent, "row", pairs(edges, rounds, depth == 0 and k == 0))
                    for _, b in edges:
                        held[k] = jnp.where(chip == b, came[n, k], held[k])
                k = step - deepest
                if k >= 0:
                    if k == last and done is not None:
                        held[k] = after(held[k], done)
                    pieces[k] = (held[k], lax.ppermute(held[k], "row", swap))
                    for batch in batches:
                        if k == batch[-1]:
                            ready = [p for b in batch for p in pieces[b]]
                            shares, extra = gram(groups, meta, met, values, ready, done is None)
                            if extra:
                                done, values = extra
                            parts += exchange(shares)
            return total_of(groups, parts, PANEL * width)

        return run

    return lax.switch(owner >> 1, [from_chip(source) for source in range(chips)], meta, met, green, start, *rest)


def solution(mesh):
    in_specs = (P("grp", "row"), P("grp", "row"), P("grp"), P(), P("grp"), P())
    out_specs = P(("row", "grp"), None)
    body = functools.partial(on_device, mesh.shape["grp"], mesh.shape["row"])
    return jax.shard_map(body, mesh=mesh, in_specs=in_specs, out_specs=out_specs, check_vma=False)
```

```python
import functools
import jax
import jax.numpy as jnp
from jax import lax
from jax.experimental import pallas as pl
from jax.experimental.pallas import tpu as pltpu
from jax.sharding import PartitionSpec as P

PANEL = 4
CHUNKS = ((0,), (1,), (2,), (3,))
BATCHES = ((0, 1), (2, 3))
ALLPREP = False
STEP = 4
SWAPPED = True
FULL = True
VMEM_LIMIT = 16 * 1024 * 1024
PREP_LIMIT = 60 * 1024 * 1024


def whole_vmem():
    return pl.BlockSpec(memory_space=pltpu.VMEM)


def smem():
    return pl.BlockSpec(memory_space=pltpu.SMEM)


def prep_body(chunks, lane, width, panel, fp_hbm, set_hbm, sw_hbm, scale_hbm, green_hbm, *refs):
    outs, (fp, sets, sw, scale, green, sems) = refs[: 2 * len(chunks)], refs[2 * len(chunks) :]
    blocks, pblocks = fp_hbm.shape
    half_blocks = pblocks // 2
    low = chunks[0][0]
    first = lax.rem(panel[0] * PANEL, blocks)
    at = pl.ds(pl.multiple_of((first + low) * width, width), green.shape[1])
    copies = [
        pltpu.make_async_copy(source, target, sems.at[n])
        for n, (source, target) in enumerate(
            ((fp_hbm, fp), (set_hbm, sets), (sw_hbm, sw), (scale_hbm, scale), (green_hbm.at[:, at], green))
        )
    ]
    mine = lax.axis_index(lane) == panel[0] * PANEL // blocks

    @pl.when(mine)
    def _():
        for copy in copies:
            copy.start()
        for copy in copies:
            copy.wait()
        core = lax.axis_index(lane) & 1
        for side in (1, 0):
            base = (core if side == 0 else 1 - core) * half_blocks
            for i in range(half_blocks):
                weight = scale[pl.ds(base + i, 1), :] * sw[sets[base + i]]
                rows = pl.ds(pl.multiple_of((base + i) * width, width), width)
                for n, cols in enumerate(chunks):
                    for m, col in enumerate(cols):
                        block = green[rows, (col - low) * width : (col - low + 1) * width]
                        value = (block.T.astype(jnp.float32) * weight).astype(jnp.bfloat16)
                        keep = fp[first + col, base + i] != 0
                        to = (slice(m * width, (m + 1) * width), slice(i * width, (i + 1) * width))
                        outs[2 * n + side][to] = jnp.where(keep, value, jnp.zeros_like(value))

    @pl.when(jnp.logical_not(mine))
    def _():
        for out in outs:
            out[...] = jnp.zeros_like(out)


def prep(limit, chunks, lane, panel_index, footprint, set_index, set_weight, scale, green):
    rows = green.shape[0]
    width = rows // footprint.shape[1]
    count = sum(len(cols) for cols in chunks)
    shapes = [jax.ShapeDtypeStruct((len(cols) * width, rows // 2), jnp.bfloat16) for cols in chunks for _ in range(2)]
    return pl.pallas_call(
        functools.partial(prep_body, chunks, lane, width),
        in_specs=[smem()] + [pl.BlockSpec(memory_space=pltpu.HBM)] * 5,
        out_specs=[whole_vmem()] * len(shapes),
        out_shape=shapes,
        scratch_shapes=[
            pltpu.SMEM(footprint.shape, jnp.int32),
            pltpu.SMEM(set_index.shape, jnp.int32),
            pltpu.SMEM(set_weight.shape, jnp.float32),
            pltpu.VMEM(scale.shape, jnp.float32),
            pltpu.VMEM((rows, count * width), jnp.bfloat16),
            pltpu.SemaphoreType.DMA((5,)),
        ],
        compiler_params=pltpu.CompilerParams(vmem_limit_bytes=limit),
        name="weigh_panel",
    )(panel_index, footprint, set_index, set_weight, scale, green)


def gram_body(shares, count, width, fresh, meta, fp_ref, green_ref, *refs):
    pieces, outs, total_ref = refs[:count], refs[count:-1], refs[-1]
    core, group = meta[0], meta[1]
    rows, cols = green_ref.shape
    half = rows // 2
    step = STEP * width
    masked_ref = green_ref
    if fresh:
        outs, done_ref, masked_ref = outs[:-2], outs[-2], outs[-1]
        done_ref[...] = jnp.zeros_like(done_ref)

    @pl.loop(0, cols // step)
    def _(n):
        here = pl.ds(pl.multiple_of(n * step, step), step)
        if fresh:
            for i in range(rows // width):
                for j in range(step // width):
                    at = (slice(i * width, (i + 1) * width), pl.ds(pl.multiple_of(n * step + j * width, width), width))
                    block = green_ref[at]
                    masked_ref[at] = jnp.where(fp_ref[n * (step // width) + j, i] != 0, block, jnp.zeros_like(block))
        total = 0.0
        for side in range(2):
            at = pl.ds(pl.multiple_of((core if side == 0 else 1 - core) * half, half), half)
            left = jnp.concatenate([p[...] for p in pieces[side::2]], 0)
            total += jnp.dot(left, masked_ref[at, here], preferred_element_type=jnp.float32)
        total_ref[:, here] = total

    share = cols // shares
    for s in range(len(outs)):
        if len(outs) > 1:
            outs[s][...] = total_ref[:, pl.ds(pl.multiple_of((group ^ s) * share, share), share)].astype(outs[s].dtype)
        else:
            outs[s][...] = total_ref[...]


def gram(shares, meta, footprint, green, pieces, fresh):
    rows, unknowns = green.shape
    width = rows // footprint.shape[1]
    share, wide = unknowns // shares, sum(p.shape[0] for p in pieces[::2])
    apart = share % width == 0
    shapes = [jax.ShapeDtypeStruct((wide, share), jnp.float32 if s == 0 else jnp.bfloat16) for s in range(shares)]
    extra = [jax.ShapeDtypeStruct((8, rows // 2), jnp.bfloat16), jax.ShapeDtypeStruct(green.shape, green.dtype)]
    all_shapes = (shapes if apart else [jax.ShapeDtypeStruct((wide, unknowns), jnp.float32)]) + (extra if fresh else [])
    out = pl.pallas_call(
        functools.partial(gram_body, shares, len(pieces), width, fresh),
        in_specs=[smem()] * 2 + [whole_vmem()] * (1 + len(pieces)),
        out_specs=[whole_vmem()] * len(all_shapes),
        out_shape=all_shapes,
        scratch_shapes=[pltpu.VMEM((wide, unknowns), jnp.float32)],
        compiler_params=pltpu.CompilerParams(vmem_limit_bytes=VMEM_LIMIT),
        name="partial_gram",
    )(meta, footprint, green, *pieces)
    count = shares if apart else 1
    parts, rest = out[:count], out[count:]
    if not apart:
        parts = [
            lax.dynamic_slice_in_dim(out[0], (meta[1] ^ s) * share, share, 1).astype(shapes[s].dtype) for s in range(shares)
        ]
    return list(parts), rest


def sum_body(shares, *refs):
    out_ref, parts = refs[-1], refs[:-1]
    at = 0
    for k in range(0, len(parts), shares):
        total = parts[k][...]
        for s in range(1, shares):
            total += parts[k + s][...].astype(jnp.float32)
        out_ref[:, at : at + total.shape[0]] = total.T
        at += total.shape[0]


def total_of(shares, parts, panel_cols):
    share = parts[0].shape[1]
    if share % 128:
        return jnp.concatenate([sum(p.astype(jnp.float32) for p in parts[k : k + shares]) for k in range(0, len(parts), shares)]).T
    return pl.pallas_call(
        functools.partial(sum_body, shares),
        in_specs=[whole_vmem()] * len(parts),
        out_specs=whole_vmem(),
        out_shape=jax.ShapeDtypeStruct((share, panel_cols), jnp.float32),
        compiler_params=pltpu.CompilerParams(vmem_limit_bytes=VMEM_LIMIT),
        name="sum_groups",
    )(*parts)


def spread(owner, chips):
    levels = {}

    def serve(source, run, depth):
        if not run:
            return
        middle = run[len(run) // 2] if len(run) > 2 else run[0]
        levels.setdefault(depth, []).append((source, middle))
        at = run.index(middle)
        serve(middle, run[:at][::-1], depth + 1)
        serve(middle, run[at + 1 :], depth + 1)

    serve(owner, list(range(owner + 1, chips)), 0)
    serve(owner, list(range(owner - 1, -1, -1)), 0)
    rounds = []
    for depth in sorted(levels):
        left = levels[depth]
        while left:
            used, later, now = set(), [], []
            for edge in left:
                (later if edge[0] in used else now).append(edge)
                used.add(edge[0])
            rounds.append((depth, now))
            left = later
    return rounds


def links(edge):
    a, b = edge
    return {(c, c + 1) for c in range(a, b)} | {(c + 1, c) for c in range(b, a)}


def pairs(edges, rounds, first):
    forth = [(2 * a + c, 2 * b + c) for a, b in edges for c in range(2)]
    taken = set().union(*(links(e) for _, some in rounds for e in some))
    back = set().union(*(links((b, a)) for a, b in edges))
    busy = [c for e in edges for c in e]
    if not FULL or len(set(busy)) < len(busy) or (back & taken and not first):
        return forth
    lanes = 2 * (1 + max(c for _, some in rounds for e in some for c in e))
    rest = [(r, r ^ 1) for r in range(lanes) if r >> 1 not in busy]
    return forth + [(b, a) for a, b in forth] + rest


def after(value, *zeros):
    for zero in zeros:
        value = value + zero[:1]
    return value


def on_device(groups, lanes, green, footprint, set_index, set_weight, pixel_scale, panel_index):
    rows, cols = green.shape
    pblocks, blocks = footprint.shape
    width = rows // pblocks
    half = rows // 2
    chips = lanes // 2
    row = lax.axis_index("row")
    core, chip = row & 1, row >> 1
    meta = jnp.stack([core, lax.axis_index("grp")])
    owner = (panel_index[0] * PANEL) // blocks
    swap = [(r, r ^ 1) for r in range(lanes)]
    met = footprint.T
    small = ("row", panel_index, met, set_index, set_weight, pixel_scale.reshape(pblocks, width), green)
    chunks = CHUNKS if chips <= 4 else ((0, 1, 2, 3),)
    batches = BATCHES if len(chunks) == len(CHUNKS) else ((0,),)
    last = len(chunks) - 1

    weighed = prep(PREP_LIMIT, chunks[:2], *small)
    own, other = weighed[:2]
    start = jnp.where(row == owner, own, lax.ppermute(other, "row", swap))
    rest = weighed[2:]

    def exchange(shares):
        return [shares[0]] + [
            lax.ppermute(shares[s], "grp", [(g, g ^ s) for g in range(groups)]) for s in range(1, groups)
        ]

    def from_chip(source):
        rounds = spread(source, chips)
        if SWAPPED and len(rounds) == 3 and rounds[1][0] == rounds[2][0]:
            rounds = [rounds[0], rounds[2], rounds[1]]
        deepest = rounds[-1][0]
        parent = {b: n for n, (_, edges) in enumerate(rounds) for _, b in edges}

        def run(meta, panel_index, met, set_index, set_weight, scale, green, start, *rest):
            sources = [start]
            if last:
                rest = [*rest, *prep(VMEM_LIMIT, chunks[2:], "row", panel_index, met, set_index, set_weight, scale, green)]
            for k in range(last):
                sources.append(jnp.where(row == owner, rest[2 * k], lax.ppermute(rest[2 * k + 1], "row", swap)))
            came, held, pieces, parts = {}, list(sources), {}, []
            done, values = None, green
            for step in range(len(chunks) + deepest):
                for n, (depth, edges) in reversed(list(enumerate(rounds))):
                    k = step - depth
                    if not 0 <= k <= last:
                        continue
                    if depth == 0:
                        sent = sources[k]
                    else:
                        sent = came[parent[edges[0][0]], k]
                        for a, _ in edges[1:]:
                            sent = jnp.where(chip == a, came[parent[a], k], sent)
                    came[n, k] = lax.ppermute(sent, "row", pairs(edges, rounds, (depth == 0 and k == 0) or (depth > 0 and k == last > 0)))
                    for _, b in edges:
                        held[k] = jnp.where(chip == b, came[n, k], held[k])
                k = step - deepest
                if k >= 0:
                    if k == last and done is not None:
                        held[k] = after(held[k], done)
                    pieces[k] = (held[k], lax.ppermute(held[k], "row", swap))
                    for batch in batches:
                        if k == batch[-1]:
                            ready = [p for b in batch for p in pieces[b]]
                            shares, extra = gram(groups, meta, met, values, ready, done is None)
                            if extra:
                                done, values = extra
                            parts += exchange(shares)
            return total_of(groups, parts, PANEL * width)

        return run

    return lax.switch(owner >> 1, [from_chip(source) for source in range(chips)], meta, *small[1:], start, *rest)


def solution(mesh):
    in_specs = (P("grp", "row"), P("grp", "row"), P("grp"), P(), P("grp"), P())
    out_specs = P(("row", "grp"), None)
    body = functools.partial(on_device, mesh.shape["grp"], mesh.shape["row"])
    return jax.shard_map(body, mesh=mesh, in_specs=in_specs, out_specs=out_specs, check_vma=False)
```

```python
import functools
import jax
import jax.numpy as jnp
from jax import lax
from jax.experimental import pallas as pl
from jax.experimental.pallas import tpu as pltpu
from jax.sharding import PartitionSpec as P

PANEL = 4
CHUNKS = ((0,), (1,), (2,), (3,))
BATCHES = ((0, 1), (2, 3))
ALLPREP = False
STEP = 4
SWAPPED = True
FULL = True
VMEM_LIMIT = 16 * 1024 * 1024
PREP_LIMIT = 60 * 1024 * 1024


def whole_vmem():
    return pl.BlockSpec(memory_space=pltpu.VMEM)


def smem():
    return pl.BlockSpec(memory_space=pltpu.SMEM)


def prep_body(chunks, lane, width, panel, fp_hbm, set_hbm, sw_hbm, scale_hbm, green_hbm, *refs):
    outs, (fp, sets, sw, scale, green, sems) = refs[: 2 * len(chunks)], refs[2 * len(chunks) :]
    blocks, pblocks = fp_hbm.shape
    half_blocks = pblocks // 2
    low = chunks[0][0]
    first = lax.rem(panel[0] * PANEL, blocks)
    at = pl.ds(pl.multiple_of((first + low) * width, width), green.shape[1])
    copies = [
        pltpu.make_async_copy(source, target, sems.at[n])
        for n, (source, target) in enumerate(
            ((fp_hbm, fp), (set_hbm, sets), (sw_hbm, sw), (scale_hbm, scale), (green_hbm.at[:, at], green))
        )
    ]
    mine = lax.axis_index(lane) == panel[0] * PANEL // blocks

    @pl.when(mine)
    def _():
        for copy in copies:
            copy.start()
        for copy in copies:
            copy.wait()
        core = lax.axis_index(lane) & 1
        for side in (1, 0):
            base = (core if side == 0 else 1 - core) * half_blocks
            for i in range(half_blocks):
                weight = scale[pl.ds(base + i, 1), :] * sw[sets[base + i]]
                rows = pl.ds(pl.multiple_of((base + i) * width, width), width)
                for n, cols in enumerate(chunks):
                    for m, col in enumerate(cols):
                        block = green[rows, (col - low) * width : (col - low + 1) * width]
                        value = (block.T.astype(jnp.float32) * weight).astype(jnp.bfloat16)
                        keep = fp[first + col, base + i] != 0
                        to = (slice(m * width, (m + 1) * width), slice(i * width, (i + 1) * width))
                        outs[2 * n + side][to] = jnp.where(keep, value, jnp.zeros_like(value))

    @pl.when(jnp.logical_not(mine))
    def _():
        for out in outs:
            out[...] = jnp.zeros_like(out)


def prep(limit, chunks, lane, panel_index, footprint, set_index, set_weight, scale, green):
    rows = green.shape[0]
    width = rows // footprint.shape[1]
    count = sum(len(cols) for cols in chunks)
    shapes = [jax.ShapeDtypeStruct((len(cols) * width, rows // 2), jnp.bfloat16) for cols in chunks for _ in range(2)]
    return pl.pallas_call(
        functools.partial(prep_body, chunks, lane, width),
        in_specs=[smem()] + [pl.BlockSpec(memory_space=pltpu.HBM)] * 5,
        out_specs=[whole_vmem()] * len(shapes),
        out_shape=shapes,
        scratch_shapes=[
            pltpu.SMEM(footprint.shape, jnp.int32),
            pltpu.SMEM(set_index.shape, jnp.int32),
            pltpu.SMEM(set_weight.shape, jnp.float32),
            pltpu.VMEM(scale.shape, jnp.float32),
            pltpu.VMEM((rows, count * width), jnp.bfloat16),
            pltpu.SemaphoreType.DMA((5,)),
        ],
        compiler_params=pltpu.CompilerParams(vmem_limit_bytes=limit),
        name="weigh_panel",
    )(panel_index, footprint, set_index, set_weight, scale, green)


def gram_body(shares, count, width, fresh, meta, fp_ref, green_ref, *refs):
    pieces, outs, total_ref = refs[:count], refs[count:-1], refs[-1]
    core, group = meta[0], meta[1]
    rows, cols = green_ref.shape
    half = rows // 2
    step = STEP * width if fresh else min(2 * STEP * width, cols)
    masked_ref = green_ref
    if fresh:
        outs, done_ref, masked_ref = outs[:-2], outs[-2], outs[-1]
        done_ref[...] = jnp.zeros_like(done_ref)

    @pl.loop(0, cols // step)
    def _(n):
        here = pl.ds(pl.multiple_of(n * step, step), step)
        if fresh:
            for i in range(rows // width):
                for j in range(step // width):
                    at = (slice(i * width, (i + 1) * width), pl.ds(pl.multiple_of(n * step + j * width, width), width))
                    block = green_ref[at]
                    masked_ref[at] = jnp.where(fp_ref[n * (step // width) + j, i] != 0, block, jnp.zeros_like(block))
        total = 0.0
        for side in range(2):
            at = pl.ds(pl.multiple_of((core if side == 0 else 1 - core) * half, half), half)
            left = jnp.concatenate([p[...] for p in pieces[side::2]], 0)
            total += jnp.dot(left, masked_ref[at, here], preferred_element_type=jnp.float32)
        total_ref[:, here] = total

    share = cols // shares
    for s in range(len(outs)):
        if len(outs) > 1:
            outs[s][...] = total_ref[:, pl.ds(pl.multiple_of((group ^ s) * share, share), share)].astype(outs[s].dtype)
        else:
            outs[s][...] = total_ref[...]


def gram(shares, meta, footprint, green, pieces, fresh):
    rows, unknowns = green.shape
    width = rows // footprint.shape[1]
    share, wide = unknowns // shares, sum(p.shape[0] for p in pieces[::2])
    apart = share % width == 0
    shapes = [jax.ShapeDtypeStruct((wide, share), jnp.float32 if s == 0 else jnp.bfloat16) for s in range(shares)]
    extra = [jax.ShapeDtypeStruct((8, rows // 2), jnp.bfloat16), jax.ShapeDtypeStruct(green.shape, green.dtype)]
    all_shapes = (shapes if apart else [jax.ShapeDtypeStruct((wide, unknowns), jnp.float32)]) + (extra if fresh else [])
    out = pl.pallas_call(
        functools.partial(gram_body, shares, len(pieces), width, fresh),
        in_specs=[smem()] * 2 + [whole_vmem()] * (1 + len(pieces)),
        out_specs=[whole_vmem()] * len(all_shapes),
        out_shape=all_shapes,
        scratch_shapes=[pltpu.VMEM((wide, unknowns), jnp.float32)],
        compiler_params=pltpu.CompilerParams(vmem_limit_bytes=VMEM_LIMIT),
        name="partial_gram",
    )(meta, footprint, green, *pieces)
    count = shares if apart else 1
    parts, rest = out[:count], out[count:]
    if not apart:
        parts = [
            lax.dynamic_slice_in_dim(out[0], (meta[1] ^ s) * share, share, 1).astype(shapes[s].dtype) for s in range(shares)
        ]
    return list(parts), rest


def sum_body(shares, *refs):
    out_ref, parts = refs[-1], refs[:-1]
    at = 0
    for k in range(0, len(parts), shares):
        total = parts[k][...]
        for s in range(1, shares):
            total += parts[k + s][...].astype(jnp.float32)
        out_ref[:, at : at + total.shape[0]] = total.T
        at += total.shape[0]


def total_of(shares, parts, panel_cols):
    share = parts[0].shape[1]
    if share % 128:
        return jnp.concatenate([sum(p.astype(jnp.float32) for p in parts[k : k + shares]) for k in range(0, len(parts), shares)]).T
    return pl.pallas_call(
        functools.partial(sum_body, shares),
        in_specs=[whole_vmem()] * len(parts),
        out_specs=whole_vmem(),
        out_shape=jax.ShapeDtypeStruct((share, panel_cols), jnp.float32),
        compiler_params=pltpu.CompilerParams(vmem_limit_bytes=VMEM_LIMIT),
        name="sum_groups",
    )(*parts)


def spread(owner, chips):
    levels = {}

    def serve(source, run, depth):
        if not run:
            return
        middle = run[len(run) // 2] if len(run) > 2 else run[0]
        levels.setdefault(depth, []).append((source, middle))
        at = run.index(middle)
        serve(middle, run[:at][::-1], depth + 1)
        serve(middle, run[at + 1 :], depth + 1)

    serve(owner, list(range(owner + 1, chips)), 0)
    serve(owner, list(range(owner - 1, -1, -1)), 0)
    rounds = []
    for depth in sorted(levels):
        left = levels[depth]
        while left:
            used, later, now = set(), [], []
            for edge in left:
                (later if edge[0] in used else now).append(edge)
                used.add(edge[0])
            rounds.append((depth, now))
            left = later
    return rounds


def links(edge):
    a, b = edge
    return {(c, c + 1) for c in range(a, b)} | {(c + 1, c) for c in range(b, a)}


def pairs(edges, rounds, first):
    forth = [(2 * a + c, 2 * b + c) for a, b in edges for c in range(2)]
    taken = set().union(*(links(e) for _, some in rounds for e in some))
    back = set().union(*(links((b, a)) for a, b in edges))
    busy = [c for e in edges for c in e]
    if not FULL or len(set(busy)) < len(busy) or (back & taken and not first):
        return forth
    lanes = 2 * (1 + max(c for _, some in rounds for e in some for c in e))
    rest = [(r, r ^ 1) for r in range(lanes) if r >> 1 not in busy]
    return forth + [(b, a) for a, b in forth] + rest


def after(value, *zeros):
    for zero in zeros:
        value = value + zero[:1]
    return value


def on_device(groups, lanes, green, footprint, set_index, set_weight, pixel_scale, panel_index):
    rows, cols = green.shape
    pblocks, blocks = footprint.shape
    width = rows // pblocks
    half = rows // 2
    chips = lanes // 2
    row = lax.axis_index("row")
    core, chip = row & 1, row >> 1
    meta = jnp.stack([core, lax.axis_index("grp")])
    owner = (panel_index[0] * PANEL) // blocks
    swap = [(r, r ^ 1) for r in range(lanes)]
    met = footprint.T
    small = ("row", panel_index, met, set_index, set_weight, pixel_scale.reshape(pblocks, width), green)
    chunks = CHUNKS if chips <= 4 else ((0, 1, 2, 3),)
    batches = BATCHES if len(chunks) == len(CHUNKS) else ((0,),)
    last = len(chunks) - 1

    weighed = prep(PREP_LIMIT, chunks[:2], *small)
    own, other = weighed[:2]
    start = jnp.where(row == owner, own, lax.ppermute(other, "row", swap))
    rest = weighed[2:]

    def exchange(shares):
        came = {s: lax.ppermute(shares[s], "grp", [(g, g ^ s) for g in range(groups)]) for s in reversed(range(1, groups))}
        return [shares[0]] + [came[s] for s in range(1, groups)]

    def from_chip(source):
        rounds = spread(source, chips)
        if SWAPPED and len(rounds) == 3 and rounds[1][0] == rounds[2][0]:
            rounds = [rounds[0], rounds[2], rounds[1]]
        deepest = rounds[-1][0]
        parent = {b: n for n, (_, edges) in enumerate(rounds) for _, b in edges}

        def run(meta, panel_index, met, set_index, set_weight, scale, green, start, *rest):
            sources = [start]
            if last:
                rest = [*rest, *prep(VMEM_LIMIT, chunks[2:], "row", panel_index, met, set_index, set_weight, scale, green)]
            for k in range(last):
                sources.append(jnp.where(row == owner, rest[2 * k], lax.ppermute(rest[2 * k + 1], "row", swap)))
            came, held, pieces, parts = {}, list(sources), {}, []
            done, values = None, green
            for step in range(len(chunks) + deepest):
                for n, (depth, edges) in reversed(list(enumerate(rounds))):
                    k = step - depth
                    if not 0 <= k <= last:
                        continue
                    if depth == 0:
                        sent = sources[k]
                    else:
                        sent = came[parent[edges[0][0]], k]
                        for a, _ in edges[1:]:
                            sent = jnp.where(chip == a, came[parent[a], k], sent)
                    came[n, k] = lax.ppermute(sent, "row", pairs(edges, rounds, (depth == 0 and k == 0) or (depth > 0 and k == last > 0)))
                    for _, b in edges:
                        held[k] = jnp.where(chip == b, came[n, k], held[k])
                k = step - deepest
                if k >= 0:
                    if k == last and done is not None:
                        held[k] = after(held[k], done)
                    pieces[k] = (held[k], lax.ppermute(held[k], "row", swap))
                    for batch in batches:
                        if k == batch[-1]:
                            ready = [p for b in batch for p in pieces[b]]
                            shares, extra = gram(groups, meta, met, values, ready, done is None)
                            if extra:
                                done, values = extra
                            parts += exchange(shares)
            return total_of(groups, parts, PANEL * width)

        return run

    return lax.switch(owner >> 1, [from_chip(source) for source in range(chips)], meta, *small[1:], start, *rest)


def solution(mesh):
    in_specs = (P("grp", "row"), P("grp", "row"), P("grp"), P(), P("grp"), P())
    out_specs = P(("row", "grp"), None)
    body = functools.partial(on_device, mesh.shape["grp"], mesh.shape["row"])
    return jax.shard_map(body, mesh=mesh, in_specs=in_specs, out_specs=out_specs, check_vma=False)
```

```python
import functools
import jax
import jax.numpy as jnp
from jax import lax
from jax.experimental import pallas as pl
from jax.experimental.pallas import tpu as pltpu
from jax.sharding import PartitionSpec as P

PANEL = 4
CHUNKS = ((0,), (1,), (2,), (3,))
BATCHES = ((0, 1), (2, 3))
ALLPREP = False
STEP = 8
SWAPPED = True
FULL = True
VMEM_LIMIT = 16 * 1024 * 1024
PREP_LIMIT = 60 * 1024 * 1024


def whole_vmem():
    return pl.BlockSpec(memory_space=pltpu.VMEM)


def smem():
    return pl.BlockSpec(memory_space=pltpu.SMEM)


def prep_body(chunks, lane, width, panel, fp_hbm, set_hbm, sw_hbm, scale_hbm, green_hbm, *refs):
    outs, (fp, sets, sw, scale, green, sems) = refs[: 2 * len(chunks)], refs[2 * len(chunks) :]
    blocks, pblocks = fp_hbm.shape
    half_blocks = pblocks // 2
    low = chunks[0][0]
    first = lax.rem(panel[0] * PANEL, blocks)
    at = pl.ds(pl.multiple_of((first + low) * width, width), green.shape[1])
    copies = [
        pltpu.make_async_copy(source, target, sems.at[n])
        for n, (source, target) in enumerate(
            ((fp_hbm, fp), (set_hbm, sets), (sw_hbm, sw), (scale_hbm, scale), (green_hbm.at[:, at], green))
        )
    ]
    mine = lax.axis_index(lane) == panel[0] * PANEL // blocks

    @pl.when(mine)
    def _():
        for copy in copies:
            copy.start()
        for copy in copies:
            copy.wait()
        core = lax.axis_index(lane) & 1
        for side in (1, 0):
            base = (core if side == 0 else 1 - core) * half_blocks
            for i in range(half_blocks):
                weight = scale[pl.ds(base + i, 1), :] * sw[sets[base + i]]
                rows = pl.ds(pl.multiple_of((base + i) * width, width), width)
                for n, cols in enumerate(chunks):
                    for m, col in enumerate(cols):
                        block = green[rows, (col - low) * width : (col - low + 1) * width]
                        value = (block.T.astype(jnp.float32) * weight).astype(jnp.bfloat16)
                        keep = fp[first + col, base + i] != 0
                        to = (slice(m * width, (m + 1) * width), slice(i * width, (i + 1) * width))
                        outs[2 * n + side][to] = jnp.where(keep, value, jnp.zeros_like(value))

    @pl.when(jnp.logical_not(mine))
    def _():
        for out in outs:
            out[...] = jnp.zeros_like(out)


def prep(limit, chunks, lane, panel_index, footprint, set_index, set_weight, scale, green):
    rows = green.shape[0]
    width = rows // footprint.shape[1]
    count = sum(len(cols) for cols in chunks)
    shapes = [jax.ShapeDtypeStruct((len(cols) * width, rows // 2), jnp.bfloat16) for cols in chunks for _ in range(2)]
    return pl.pallas_call(
        functools.partial(prep_body, chunks, lane, width),
        in_specs=[smem()] + [pl.BlockSpec(memory_space=pltpu.HBM)] * 5,
        out_specs=[whole_vmem()] * len(shapes),
        out_shape=shapes,
        scratch_shapes=[
            pltpu.SMEM(footprint.shape, jnp.int32),
            pltpu.SMEM(set_index.shape, jnp.int32),
            pltpu.SMEM(set_weight.shape, jnp.float32),
            pltpu.VMEM(scale.shape, jnp.float32),
            pltpu.VMEM((rows, count * width), jnp.bfloat16),
            pltpu.SemaphoreType.DMA((5,)),
        ],
        compiler_params=pltpu.CompilerParams(vmem_limit_bytes=limit),
        name="weigh_panel",
    )(panel_index, footprint, set_index, set_weight, scale, green)


def gram_body(shares, count, width, fresh, meta, fp_ref, green_ref, *refs):
    pieces, outs, total_ref = refs[:count], refs[count:-1], refs[-1]
    core, group = meta[0], meta[1]
    rows, cols = green_ref.shape
    half = rows // 2
    step = STEP * width if fresh else min(2 * STEP * width, cols)
    masked_ref = green_ref
    if fresh:
        outs, done_ref, masked_ref = outs[:-2], outs[-2], outs[-1]
        done_ref[...] = jnp.zeros_like(done_ref)

    @pl.loop(0, cols // step)
    def _(n):
        here = pl.ds(pl.multiple_of(n * step, step), step)
        if fresh:
            for i in range(rows // width):
                for j in range(step // width):
                    at = (slice(i * width, (i + 1) * width), pl.ds(pl.multiple_of(n * step + j * width, width), width))
                    block = green_ref[at]
                    masked_ref[at] = jnp.where(fp_ref[n * (step // width) + j, i] != 0, block, jnp.zeros_like(block))
        total = 0.0
        for side in range(2):
            at = pl.ds(pl.multiple_of((core if side == 0 else 1 - core) * half, half), half)
            left = jnp.concatenate([p[...] for p in pieces[side::2]], 0)
            total += jnp.dot(left, masked_ref[at, here], preferred_element_type=jnp.float32)
        total_ref[:, here] = total

    share = cols // shares
    for s in range(len(outs)):
        if len(outs) > 1:
            outs[s][...] = total_ref[:, pl.ds(pl.multiple_of((group ^ s) * share, share), share)].astype(outs[s].dtype)
        else:
            outs[s][...] = total_ref[...]


def gram(shares, meta, footprint, green, pieces, fresh):
    rows, unknowns = green.shape
    width = rows // footprint.shape[1]
    share, wide = unknowns // shares, sum(p.shape[0] for p in pieces[::2])
    apart = share % width == 0
    shapes = [jax.ShapeDtypeStruct((wide, share), jnp.float32 if s == 0 else jnp.bfloat16) for s in range(shares)]
    extra = [jax.ShapeDtypeStruct((8, rows // 2), jnp.bfloat16), jax.ShapeDtypeStruct(green.shape, green.dtype)]
    all_shapes = (shapes if apart else [jax.ShapeDtypeStruct((wide, unknowns), jnp.float32)]) + (extra if fresh else [])
    out = pl.pallas_call(
        functools.partial(gram_body, shares, len(pieces), width, fresh),
        in_specs=[smem()] * 2 + [whole_vmem()] * (1 + len(pieces)),
        out_specs=[whole_vmem()] * len(all_shapes),
        out_shape=all_shapes,
        scratch_shapes=[pltpu.VMEM((wide, unknowns), jnp.float32)],
        compiler_params=pltpu.CompilerParams(vmem_limit_bytes=VMEM_LIMIT),
        name="partial_gram",
    )(meta, footprint, green, *pieces)
    count = shares if apart else 1
    parts, rest = out[:count], out[count:]
    if not apart:
        parts = [
            lax.dynamic_slice_in_dim(out[0], (meta[1] ^ s) * share, share, 1).astype(shapes[s].dtype) for s in range(shares)
        ]
    return list(parts), rest


def sum_body(shares, *refs):
    out_ref, parts = refs[-1], refs[:-1]
    at = 0
    for k in range(0, len(parts), shares):
        total = parts[k][...]
        for s in range(1, shares):
            total += parts[k + s][...].astype(jnp.float32)
        out_ref[:, at : at + total.shape[0]] = total.T
        at += total.shape[0]


def total_of(shares, parts, panel_cols):
    share = parts[0].shape[1]
    if share % 128:
        return jnp.concatenate([sum(p.astype(jnp.float32) for p in parts[k : k + shares]) for k in range(0, len(parts), shares)]).T
    return pl.pallas_call(
        functools.partial(sum_body, shares),
        in_specs=[whole_vmem()] * len(parts),
        out_specs=whole_vmem(),
        out_shape=jax.ShapeDtypeStruct((share, panel_cols), jnp.float32),
        compiler_params=pltpu.CompilerParams(vmem_limit_bytes=VMEM_LIMIT),
        name="sum_groups",
    )(*parts)


def spread(owner, chips):
    levels = {}

    def serve(source, run, depth):
        if not run:
            return
        middle = run[len(run) // 2] if len(run) > 2 else run[0]
        levels.setdefault(depth, []).append((source, middle))
        at = run.index(middle)
        serve(middle, run[:at][::-1], depth + 1)
        serve(middle, run[at + 1 :], depth + 1)

    serve(owner, list(range(owner + 1, chips)), 0)
    serve(owner, list(range(owner - 1, -1, -1)), 0)
    rounds = []
    for depth in sorted(levels):
        left = levels[depth]
        while left:
            used, later, now = set(), [], []
            for edge in left:
                (later if edge[0] in used else now).append(edge)
                used.add(edge[0])
            rounds.append((depth, now))
            left = later
    return rounds


def links(edge):
    a, b = edge
    return {(c, c + 1) for c in range(a, b)} | {(c + 1, c) for c in range(b, a)}


def pairs(edges, rounds, first):
    forth = [(2 * a + c, 2 * b + c) for a, b in edges for c in range(2)]
    taken = set().union(*(links(e) for _, some in rounds for e in some))
    back = set().union(*(links((b, a)) for a, b in edges))
    busy = [c for e in edges for c in e]
    if not FULL or len(set(busy)) < len(busy) or (back & taken and not first):
        return forth
    lanes = 2 * (1 + max(c for _, some in rounds for e in some for c in e))
    rest = [(r, r ^ 1) for r in range(lanes) if r >> 1 not in busy]
    return forth + [(b, a) for a, b in forth] + rest


def after(value, *zeros):
    for zero in zeros:
        value = value + zero[:1]
    return value


def on_device(groups, lanes, green, footprint, set_index, set_weight, pixel_scale, panel_index):
    rows, cols = green.shape
    pblocks, blocks = footprint.shape
    width = rows // pblocks
    half = rows // 2
    chips = lanes // 2
    row = lax.axis_index("row")
    core, chip = row & 1, row >> 1
    meta = jnp.stack([core, lax.axis_index("grp")])
    owner = (panel_index[0] * PANEL) // blocks
    swap = [(r, r ^ 1) for r in range(lanes)]
    met = footprint.T
    small = ("row", panel_index, met, set_index, set_weight, pixel_scale.reshape(pblocks, width), green)
    chunks = CHUNKS if chips <= 4 else ((0, 1, 2, 3),)
    batches = BATCHES if len(chunks) == len(CHUNKS) else ((0,),)
    last = len(chunks) - 1

    weighed = prep(PREP_LIMIT, chunks[:2], *small)
    own, other = weighed[:2]
    start = jnp.where(row == owner, own, lax.ppermute(other, "row", swap))
    rest = weighed[2:]

    def exchange(shares):
        came = {s: lax.ppermute(shares[s], "grp", [(g, g ^ s) for g in range(groups)]) for s in reversed(range(1, groups))}
        return [shares[0]] + [came[s] for s in range(1, groups)]

    def from_chip(source):
        rounds = spread(source, chips)
        if SWAPPED and len(rounds) == 3 and rounds[1][0] == rounds[2][0]:
            rounds = [rounds[0], rounds[2], rounds[1]]
        deepest = rounds[-1][0]
        parent = {b: n for n, (_, edges) in enumerate(rounds) for _, b in edges}

        def run(meta, panel_index, met, set_index, set_weight, scale, green, start, *rest):
            sources = [start]
            if last:
                rest = [*rest, *prep(VMEM_LIMIT, chunks[2:], "row", panel_index, met, set_index, set_weight, scale, green)]
            for k in range(last):
                sources.append(jnp.where(row == owner, rest[2 * k], lax.ppermute(rest[2 * k + 1], "row", swap)))
            came, held, pieces, parts = {}, list(sources), {}, []
            done, values = None, green
            for step in range(len(chunks) + deepest):
                for n, (depth, edges) in reversed(list(enumerate(rounds))):
                    k = step - depth
                    if not 0 <= k <= last:
                        continue
                    if depth == 0:
                        sent = sources[k]
                    else:
                        sent = came[parent[edges[0][0]], k]
                        for a, _ in edges[1:]:
                            sent = jnp.where(chip == a, came[parent[a], k], sent)
                    came[n, k] = lax.ppermute(sent, "row", pairs(edges, rounds, (depth == 0 and k == 0) or (depth > 0 and k == last > 0)))
                    for _, b in edges:
                        held[k] = jnp.where(chip == b, came[n, k], held[k])
                k = step - deepest
                if k >= 0:
                    if k == last and done is not None:
                        held[k] = after(held[k], done)
                    pieces[k] = (held[k], lax.ppermute(held[k], "row", swap))
                    for batch in batches:
                        if k == batch[-1]:
                            ready = [p for b in batch for p in pieces[b]]
                            shares, extra = gram(groups, meta, met, values, ready, done is None)
                            if extra:
                                done, values = extra
                            parts += exchange(shares)
            return total_of(groups, parts, PANEL * width)

        return run

    return lax.switch(owner >> 1, [from_chip(source) for source in range(chips)], meta, *small[1:], start, *rest)


def solution(mesh):
    in_specs = (P("grp", "row"), P("grp", "row"), P("grp"), P(), P("grp"), P())
    out_specs = P(("row", "grp"), None)
    body = functools.partial(on_device, mesh.shape["grp"], mesh.shape["row"])
    return jax.shard_map(body, mesh=mesh, in_specs=in_specs, out_specs=out_specs, check_vma=False)
```
